512 devices in a mesh: section: 8 (over y_lo, core), ctx: 64 (over z, y_hi, x).
Axes of the slice: x: 4, y: 8 (y_hi: 2, y_lo: 4; y = y_hi * 4 + y_lo), z: 8, core: 2. Of those that a mesh axis runs over, the one named last changes fastest.
Arguments:
- queries: bfloat16 [8, 8192, 2560], P('section', 'ctx'), may hold values from -6 to 6
- keys: bfloat16 [8192, 512], P('ctx'), may hold values from -6 to 6
- values: bfloat16 [8192, 512], P('ctx'), may hold values from -6 to 6
- cotangent: bfloat16 [8, 8192, 2560], P('section', 'ctx'), may hold values from -6 to 6
- segment_ids: int32 [8192], P('ctx'), may hold values from 0 to 95, never falling along the last dimension, each value on 1 to 256 neighbouring positions
Outputs:
- grad_queries: bfloat16 [8, 8192, 2560], P('section', 'ctx')
- grad_keys: float32 [8192, 512], P('ctx', 'section')
- grad_values: float32 [8192, 512], P('ctx', 'section')
The draws below stay inside these ranges and needn't reach their ends.
Inputs may be any that keep to these rules, and one draw needn't show every extreme that they name: `segment_ids`: ids never fall; each document covers 1 to 256 tokens, one exactly 256.
All inputs are finite; a program needn't handle non-finite values.
Results may differ from the reference program's by a relative error of at most 0.007.
Values may be sent and summed in bfloat16 or wider, within the bound.
No kernel may reach another device: no remote copies, remote signals or barrier semaphores. Data moves between devices by JAX's collectives and lax.ppermute only.
A program may use at most 64 MiB of HBM per device.

```python
import math
import jax
import jax.numpy as jnp
import numpy as np
from jax import lax

H = 20
G = 4
DH = 128
TOK_DEV = 128
DOC_SHARDS = 2
LAYERS = 8
TOKENS = 8192
DOC_MOST = 256
DOCS = 96


def draw_queries(key, part):
    key = jax.random.fold_in(key, 1)
    shape = (LAYERS, TOKENS, H * DH)
    base = jnp.clip(jax.random.normal(key, shape, jnp.float32), -6.0, 6.0)
    return base.astype(jnp.bfloat16)


def draw_keys(key, part):
    key = jax.random.fold_in(key, 2)
    shape = (TOKENS, G * DH)
    base = jnp.clip(jax.random.normal(key, shape, jnp.float32), -6.0, 6.0)
    return base.astype(jnp.bfloat16)


def levels(key, shape, pieces, low, largest):
    gain, own = 1.0, jax.random.fold_in(key, 6)
    for position, shards_of in pieces:
        steps = jnp.exp(jax.random.uniform(jax.random.fold_in(own, position), (shards_of,), jnp.float32, low / len(pieces), largest / len(pieces)))
        gain = gain * jnp.repeat(steps, shape[position] // shards_of).reshape([-1 if axis == position else 1 for axis in range(len(shape))])
    return gain


def profile(count, total, bound, slope):
    portions = [(1 << 20) // math.isqrt(rank ** slope) + 1 for rank in range(2, count + 1)]
    rest, holding = total - bound - (count - 1), [1] * (count - 1)
    while rest > 0:
        free = [i for i in range(count - 1) if holding[i] < bound]
        pool, left = sum([portions[i] for i in free]), rest
        for i in free:
            extra = min(bound - holding[i], max(1, left * portions[i] // pool), rest)
            holding[i] = holding[i] + extra
            rest = rest - extra
    return np.array([bound] + holding)


def uneven(stream_key, count, total, limit, slope):
    if count == 2:
        one = jax.random.randint(stream_key, (), max(1, total - limit), min(limit, total - 1) + 1)
        return jnp.stack([one, total - one])
    sizes = jnp.asarray(profile(count, total, limit, slope), jnp.int32)
    twos = (count - 1) // 2
    source_of, taker = sizes[1:1 + 2 * twos:2], sizes[2:2 + 2 * twos:2]
    room = jnp.minimum(source_of - 1, limit - taker)
    passed = jax.random.randint(jax.random.fold_in(stream_key, 1), (twos,), 0, 1 << 20) % (room + 1)
    sizes = sizes.at[1:1 + 2 * twos:2].set(source_of - passed).at[2:2 + 2 * twos:2].set(taker + passed)
    return sizes[jax.random.permutation(jax.random.fold_in(stream_key, 2), count)]


def bell_draw(key, shape, scale, bound, pieces=(), kind=jnp.bfloat16):
    result = jax.random.normal(key, shape, jnp.float32) * scale
    if len(pieces) > 0:
        result = levels(key, shape, pieces, -0.22, 0.18) * result
    return jnp.clip(result, min=-bound, max=bound).astype(kind)


def setup_inputs(seed: int = 0) -> dict:
    arg_keys = jax.random.split(jax.random.key(seed), 6)
    queries = draw_queries(jax.random.fold_in(arg_keys[5], 71), 0)
    keys = draw_keys(jax.random.fold_in(arg_keys[5], 71), 0)
    values = bell_draw(arg_keys[2], (TOKENS, G * DH), 1.0, 6.0, ((0, 64),))
    cotangent = bell_draw(arg_keys[3], (LAYERS, TOKENS, H * DH), 1.0, 6.0, ((0, 8), (1, 64)))
    segment_ids = jnp.searchsorted(jnp.cumsum(uneven(arg_keys[4], DOCS, TOKENS, DOC_MOST, 2)), jnp.arange(TOKENS), side="right").astype(jnp.int32)
    return {"queries": queries, "keys": keys, "values": values, "cotangent": cotangent, "segment_ids": segment_ids}


def by_group(rows, groups):
    count, width = rows.shape
    head_ratio = width // (groups * DH)
    return rows.reshape(count, groups, head_ratio, DH).transpose(1, 2, 0, 3).reshape(groups, head_ratio * count, DH)


def reference(queries, keys, values, cotangent, segment_ids):
    score_scale = DH ** -0.5
    head_ratio = H // G
    pad_rows = DOC_SHARDS * TOK_DEV
    window = (DOC_SHARDS + 1) * TOK_DEV
    key_pad = jnp.concatenate([jnp.zeros((pad_rows, G * DH), keys.dtype), keys], 0)
    value_pad = jnp.concatenate([jnp.zeros((pad_rows, G * DH), values.dtype), values], 0)
    seg_pad = jnp.concatenate([jnp.full((pad_rows,), -1, jnp.int32), segment_ids.astype(jnp.int32)], 0)
    zero_index = jnp.zeros((), jnp.int32)

    def layer_pass(carry, layer_data):
        query_layer, grad_layer = layer_data

        def block_pass(inner, block_index):
            key_acc, value_acc = inner
            row_start = (block_index * TOK_DEV).astype(jnp.int32)
            query_rows = by_group(lax.dynamic_slice_in_dim(query_layer, row_start, TOK_DEV, 0), G).astype(jnp.float32)
            grad_rows = by_group(lax.dynamic_slice_in_dim(grad_layer, row_start, TOK_DEV, 0), G).astype(jnp.float32)
            key_block = lax.dynamic_slice_in_dim(key_pad, row_start, window, 0)
            value_block = lax.dynamic_slice_in_dim(value_pad, row_start, window, 0)
            key_seg = lax.dynamic_slice_in_dim(seg_pad, row_start, window, 0)
            key_rows = key_block.reshape(window, G, DH).transpose(1, 0, 2).astype(jnp.float32)
            value_rows = value_block.reshape(window, G, DH).transpose(1, 0, 2).astype(jnp.float32)
            scores = jnp.einsum("grd,gkd->grk", query_rows, key_rows) * score_scale
            row_pos = row_start + jnp.tile(jnp.arange(TOK_DEV, dtype=jnp.int32), head_ratio)
            row_seg = jnp.tile(lax.dynamic_slice_in_dim(segment_ids, row_start, TOK_DEV, 0), head_ratio)
            key_pos = row_start - pad_rows + jnp.arange(window, dtype=jnp.int32)
            allowed = (row_seg[:, None] == key_seg[None, :]) & (key_pos[None, :] <= row_pos[:, None])
            row_max = jnp.max(jnp.where(allowed, scores, -jnp.inf), -1, keepdims=True)
            row_sum = jnp.sum(jnp.where(allowed, jnp.exp(scores - row_max), 0.0), -1, keepdims=True)
            log_total = row_max + jnp.log(row_sum)
            probs = jnp.where(allowed, jnp.exp(scores - log_total), 0.0)
            probs_low = lax.optimization_barrier(probs.astype(jnp.bfloat16)).astype(jnp.float32)
            output_rows = jnp.einsum("grk,gkd->grd", probs_low, value_rows)
            row_dot = jnp.sum(grad_rows * output_rows, -1, keepdims=True)
            grad_probs = jnp.einsum("grd,gkd->grk", grad_rows, value_rows)
            grad_scores = probs * (grad_probs - row_dot)
            scaled_low = lax.optimization_barrier((grad_scores * score_scale).astype(jnp.bfloat16)).astype(jnp.float32)
            grad_query = jnp.einsum("grk,gkd->grd", scaled_low, key_rows)
            grad_key = jnp.einsum("grk,grd->gkd", scaled_low, query_rows).transpose(1, 0, 2).reshape(window, G * DH)
            grad_value = jnp.einsum("grk,grd->gkd", probs_low, grad_rows).transpose(1, 0, 2).reshape(window, G * DH)
            key_acc = lax.dynamic_update_slice(key_acc, lax.dynamic_slice_in_dim(key_acc, row_start, window, 0) + grad_key, (row_start, zero_index))
            value_acc = lax.dynamic_update_slice(value_acc, lax.dynamic_slice_in_dim(value_acc, row_start, window, 0) + grad_value, (row_start, zero_index))
            query_out = grad_query.reshape(G, head_ratio, TOK_DEV, DH).transpose(2, 0, 1, 3).reshape(TOK_DEV, H * DH)
            return (key_acc, value_acc), query_out.astype(jnp.bfloat16)

        carry, query_blocks = lax.scan(block_pass, carry, jnp.arange(TOKENS // TOK_DEV, dtype=jnp.int32))
        return carry, query_blocks.reshape(TOKENS, H * DH)

    start_acc = jnp.zeros((TOKENS + pad_rows, G * DH), jnp.float32)
    (key_acc, value_acc), grad_queries = lax.scan(layer_pass, (start_acc, start_acc), (queries, cotangent))
    return grad_queries, key_acc[pad_rows:], value_acc[pad_rows:]
```

```python
import jax
import jax.numpy as jnp
from jax import lax
from jax.experimental import pallas as pl
from jax.experimental.pallas import tpu as pltpu
from jax.sharding import PartitionSpec as P

DH = 128
TOK = 128
GROUPS = 4
RATIO = 5
ROW = 4
ID_ROWS = 16
SCALE = DH ** (-0.5)
LOG2E = 1.4426950408889634
NEG = -1e30
AXES = ("section", "ctx")
NT = (((1,), (1,)), ((), ()))
TN = (((0,), (0,)), ((), ()))


def pairs(target):
    sections, cycle = lax.axis_size("section"), lax.axis_size("ctx")
    out = []
    for s in range(sections):
        for c in range(cycle):
            to = target(s, c)
            if 0 <= to[1] < cycle:
                out.append((s * cycle + c, to[0] * cycle + to[1]))
    return out


def shifted(x, by):
    sections = lax.axis_size("section")

    def target(s, c):
        mirror = (c // ROW) != ((c + by) // ROW)
        return ((sections // 2 - 1 - s // 2) * 2 + s % 2 if mirror else s, c + by)

    return lax.ppermute(x, AXES, pairs(target))


def other_core(x):
    return lax.ppermute(x, AXES, pairs(lambda s, c: (s ^ 1, c)))


def small_shift(x, by):
    return lax.ppermute(x, AXES, pairs(lambda s, c: (s, c + by)))


def attend(core_ref, ids_ref, q_ref, c_ref, k_ref, v_ref, hk_ref, hv_ref, ok_ref, ov_ref, id_ref, dq_ref, part_ref):
    group = pl.program_id(0)
    mine = core_ref[0] == group // 2
    ids = ids_ref[...].astype(jnp.float32)
    first = ids[:, 0:1]
    bound = 2 * TOK
    k_halo = jnp.where(mine, hk_ref[...], ok_ref[...])
    v_halo = jnp.where(mine, hv_ref[...], ov_ref[...])
    keys = jnp.concatenate([k_ref[...], k_halo[:TOK], k_halo[TOK:bound]], 0)
    values = jnp.concatenate([v_ref[...], v_halo[:TOK], v_halo[TOK:bound]], 0)
    row = lax.broadcasted_iota(jnp.int32, (TOK, TOK), 0)
    col = lax.broadcasted_iota(jnp.int32, (TOK, TOK), 1)
    wide = jnp.broadcast_to(ids, (TOK, TOK))
    own = jnp.where((wide.T == wide) & (row <= col), 0.0, NEG)
    biases = [own]
    rowf = row.astype(jnp.float32)
    for d in range(2):
        before = id_ref[d * ID_ROWS : d * ID_ROWS + 1, :].astype(jnp.float32)
        held = jnp.sum(jnp.where(before == first + 1.0, 1.0, 0.0), -1, keepdims=True)
        biases.append(jnp.where((wide == first) & (rowf >= TOK - held), 0.0, NEG))
    bias = jnp.concatenate(biases, 0)
    queries = jnp.concatenate([q_ref[:, h * DH : (h + 1) * DH] for h in range(RATIO)], 0)
    cots = jnp.concatenate([c_ref[:, h * DH : (h + 1) * DH] for h in range(RATIO)], 0)
    scores = lax.dot_general(keys, queries, NT, preferred_element_type=jnp.float32)
    grad_probs = lax.dot_general(values, cots, NT, preferred_element_type=jnp.float32)
    probs_low, scaled_low = [], []
    for h in range(RATIO):
        at = slice(h * TOK, (h + 1) * TOK)
        s = scores[:, at] * (SCALE * LOG2E) + bias
        e = jnp.exp2(s - jnp.max(s, 0, keepdims=True))
        p = e * (1.0 / jnp.sum(e, 0, keepdims=True))
        low = p.astype(jnp.bfloat16)
        g = grad_probs[:, at]
        dot = jnp.sum(low.astype(jnp.float32) * g, 0, keepdims=True)
        probs_low.append(low)
        scaled_low.append((p * (g - dot) * SCALE).astype(jnp.bfloat16))
    probs_low = jnp.concatenate(probs_low, 1)
    scaled_low = jnp.concatenate(scaled_low, 1)
    grad_v = jnp.dot(probs_low, cots, preferred_element_type=jnp.float32).astype(jnp.bfloat16)
    grad_k = jnp.dot(scaled_low, queries, preferred_element_type=jnp.float32).astype(jnp.bfloat16)
    grad_q = lax.dot_general(keys, scaled_low, TN, preferred_element_type=jnp.float32)
    for h in range(RATIO):
        at = slice(h * TOK, (h + 1) * TOK)
        dq_ref[:, at] = grad_q[:, at].T.astype(jnp.bfloat16)
    half = DH // 2
    part_ref[0] = jnp.concatenate([grad_k[:, :half], grad_v[:, :half]], 1)
    part_ref[1] = jnp.concatenate([grad_k[:, half:], grad_v[:, half:]], 1)


def on_device(queries, keys, values, cotangent, segment_ids):
    core = lax.axis_index("section") % 2
    groups = keys.shape[1] // DH
    width = keys.shape[1] // 2
    tok = keys.shape[0]
    ids = jnp.broadcast_to((segment_ids + 1).astype(jnp.bfloat16)[None], (ID_ROWS, tok))
    ids = jnp.pad(ids, ((0, 0), (0, 2 * width - tok)))
    mine = jnp.concatenate(
        [
            jnp.where(core == 0, keys[:, :width], keys[:, width:]),
            jnp.where(core == 0, values[:, :width], values[:, width:]),
        ],
        1,
    )
    sent = jnp.concatenate([mine, ids], 0)
    one, two = shifted(sent, 1), shifted(sent, 2)
    halo = jnp.concatenate([one[:tok], two[:tok]], 0)
    halo_ids = jnp.concatenate([one[tok:, :tok], two[tok:, :tok]], 0)
    other = other_core(halo)
    per = width // DH
    grad_q, part = pl.pallas_call(
        attend,
        grid=(groups,),
        out_shape=(
            jax.ShapeDtypeStruct((tok, queries.shape[2]), jnp.bfloat16),
            jax.ShapeDtypeStruct((2 * groups, 3 * tok, DH), jnp.bfloat16),
        ),
        in_specs=[
            pl.BlockSpec(memory_space=pltpu.SMEM),
            pl.BlockSpec((1, tok), lambda g: (0, 0)),
            pl.BlockSpec((tok, RATIO * DH), lambda g: (0, g)),
            pl.BlockSpec((tok, RATIO * DH), lambda g: (0, g)),
            pl.BlockSpec((tok, DH), lambda g: (0, g)),
            pl.BlockSpec((tok, DH), lambda g: (0, g)),
            pl.BlockSpec((2 * tok, DH), lambda g: (0, g % per)),
            pl.BlockSpec((2 * tok, DH), lambda g: (0, per + g % per)),
            pl.BlockSpec((2 * tok, DH), lambda g: (0, g % per)),
            pl.BlockSpec((2 * tok, DH), lambda g: (0, per + g % per)),
            pl.BlockSpec((2 * ID_ROWS, tok), lambda g: (0, 0)),
        ],
        out_specs=(
            pl.BlockSpec((tok, RATIO * DH), lambda g: (0, g)),
            pl.BlockSpec((2, 3 * tok, DH), lambda g: (g, 0, 0)),
        ),
        compiler_params=pltpu.CompilerParams(vmem_limit_bytes=40 * 1024 * 1024),
        name="attend",
    )(
        core.astype(jnp.int32).reshape(1),
        segment_ids.reshape(1, tok),
        queries[0],
        cotangent[0],
        keys,
        values,
        halo,
        halo,
        other,
        other,
        halo_ids,
    )
    shares = lax.all_to_all(part, "section", 0, 0)
    total = jnp.sum(shares.astype(jnp.float32), 0)
    back_one = small_shift(total[tok : 2 * tok].astype(jnp.bfloat16), -1)
    back_two = small_shift(total[2 * tok :].astype(jnp.bfloat16), -2)
    total = total[:tok] + back_one.astype(jnp.float32) + back_two.astype(jnp.float32)
    half = DH // 2
    return (grad_q[None], total[:, :half], total[:, half:])


def solution(mesh):
    placed = (
        P("section", "ctx", None),
        P("ctx", None),
        P("ctx", None),
        P("section", "ctx", None),
        P("ctx"),
    )
    return jax.shard_map(
        on_device,
        mesh=mesh,
        in_specs=placed,
        out_specs=(P("section", "ctx", None), P("ctx", "section"), P("ctx", "section")),
        check_vma=False,
    )
```

```python
import jax
import jax.numpy as jnp
from jax import lax
from jax.experimental import pallas as pl
from jax.experimental.pallas import tpu as pltpu
from jax.sharding import PartitionSpec as P

DH = 128
TOK = 128
RATIO = 5
WIDE = RATIO * DH
ROW = 4
ID_ROWS = 16
SCALE = DH ** (-0.5)
LOG2E = 1.4426950408889634
NEG = -1e30
AXES = ("section", "ctx")
NT = (((1,), (1,)), ((), ()))
TN = (((0,), (0,)), ((), ()))


def permuted(x, target):
    sections, cycle = lax.axis_size("section"), lax.axis_size("ctx")
    found = []
    for s in range(sections):
        for c in range(cycle):
            to = target(s, c)
            if 0 <= to[1] < cycle:
                found.append((s * cycle + c, to[0] * cycle + to[1]))
    return lax.ppermute(x, AXES, found)


def shifted(x, by):
    def target(s, c):
        leaves = (c // ROW) != ((c + by) // ROW)
        return ((3 - s // 2) * 2 + s % 2 if leaves else s, c + by)

    return permuted(x, target)


def other_core(x):
    return permuted(x, lambda s, c: (s ^ 1, c))


def group_of(core, slot):
    return core + slot * (3 - 2 * core)


def to_owner(x, step):
    def target(s, c):
        share = (s // 2) ^ step
        return (group_of(s % 2, share // 2) * 2 + share % 2, c)

    return permuted(x, target)


def attend(
    place_ref, ids_ref, q_ref, c_ref, oq_ref, oc_ref, k_ref, v_ref, k1_ref, v1_ref, k2_ref, v2_ref,
    id1_ref, id2_ref, dq_ref, odq_ref, part_ref,
):
    slot = pl.program_id(0)
    ids = ids_ref[...].astype(jnp.float32)
    first = ids[:, 0:1]
    keys = jnp.concatenate([k_ref[...], k1_ref[...], k2_ref[...]], 0)
    values = jnp.concatenate([v_ref[...], v1_ref[...], v2_ref[...]], 0)
    row = lax.broadcasted_iota(jnp.int32, (TOK, TOK), 0)
    col = lax.broadcasted_iota(jnp.int32, (TOK, TOK), 1)
    wide = jnp.broadcast_to(ids, (TOK, TOK))
    biases = [jnp.where((wide.T == wide) & (row <= col), 0.0, NEG)]
    for id_ref in (id1_ref, id2_ref):
        before = id_ref[0:1, :].astype(jnp.float32)
        held = jnp.sum(jnp.where(before == first + 1.0, 1.0, 0.0), -1, keepdims=True)
        biases.append(jnp.where((wide == first) & (row.astype(jnp.float32) >= TOK - held), 0.0, NEG))
    bias = jnp.concatenate(biases, 0)
    grad_k = jnp.zeros((3 * TOK, DH), jnp.float32)
    grad_v = jnp.zeros((3 * TOK, DH), jnp.float32)
    for layer_q, layer_c, out in ((q_ref, c_ref, dq_ref), (oq_ref, oc_ref, odq_ref)):
        queries = jnp.concatenate([layer_q[:, h * DH : (h + 1) * DH] for h in range(RATIO)], 0)
        cots = jnp.concatenate([layer_c[:, h * DH : (h + 1) * DH] for h in range(RATIO)], 0)
        scores = lax.dot_general(keys, queries, NT, preferred_element_type=jnp.float32)
        grad_probs = lax.dot_general(values, cots, NT, preferred_element_type=jnp.float32)
        probs_low, scaled_low = [], []
        for h in range(RATIO):
            at = slice(h * TOK, (h + 1) * TOK)
            s = scores[:, at] * (SCALE * LOG2E) + bias
            e = jnp.exp2(s - jnp.max(s, 0, keepdims=True))
            p = e * (1.0 / jnp.sum(e, 0, keepdims=True))
            low = p.astype(jnp.bfloat16)
            g = grad_probs[:, at]
            dot = jnp.sum(low.astype(jnp.float32) * g, 0, keepdims=True)
            probs_low.append(low)
            scaled_low.append((p * (g - dot) * SCALE).astype(jnp.bfloat16))
        probs_low = jnp.concatenate(probs_low, 1)
        scaled_low = jnp.concatenate(scaled_low, 1)
        grad_v += jnp.dot(probs_low, cots, preferred_element_type=jnp.float32)
        grad_k += jnp.dot(scaled_low, queries, preferred_element_type=jnp.float32)
        grad_q = lax.dot_general(keys, scaled_low, TN, preferred_element_type=jnp.float32)
        for h in range(RATIO):
            at = slice(h * TOK, (h + 1) * TOK)
            out[:, at] = grad_q[:, at].T.astype(jnp.bfloat16)
    half = DH // 2
    grad_k = grad_k.astype(jnp.bfloat16)
    grad_v = grad_v.astype(jnp.bfloat16)
    shares = (
        jnp.concatenate([grad_k[:, :half], grad_v[:, :half]], 1),
        jnp.concatenate([grad_k[:, half:], grad_v[:, half:]], 1),
    )
    for block in range(3):
        mirror = place_ref[2 + block]
        rows = slice(block * TOK, (block + 1) * TOK)
        for side in range(2):
            share = 2 * (slot ^ mirror) + side
            part_ref[share ^ place_ref[1], rows, :] = shares[side][rows]


def finish(own_ref, one_ref, two_ref, dk_ref, dv_ref):
    total = own_ref[...] + one_ref[...].astype(jnp.float32) + two_ref[...].astype(jnp.float32)
    total = total.T
    dk_ref[...] = total[: DH // 2]
    dv_ref[...] = total[DH // 2 :]


def on_device(queries, keys, values, cotangent, segment_ids):
    section, me = lax.axis_index("section"), lax.axis_index("ctx")
    core, y_lo = section % 2, section // 2
    tok = keys.shape[0]
    q, c = queries[0], cotangent[0]

    def of_core(x, unit, which):
        outer = jnp.concatenate([x[:, :unit], x[:, 3 * unit :]], 1)
        return jnp.where(which == 0, outer, x[:, unit : 3 * unit])

    ids = jnp.broadcast_to((segment_ids + 1).astype(jnp.bfloat16)[None], (ID_ROWS, tok))
    ids = jnp.pad(ids, ((0, 0), (0, 4 * DH - tok)))
    sent = jnp.concatenate([of_core(keys, DH, core), of_core(values, DH, core)], 1)
    sent = jnp.concatenate([sent, ids], 0)
    one, two = shifted(sent, 1), shifted(sent, 2)
    q, c, _ = lax.optimization_barrier((q, c, sent))
    swapped = other_core(jnp.concatenate([of_core(q, WIDE, 1 - core), of_core(c, WIDE, 1 - core)], 0))
    place = jnp.stack(
        [core, y_lo, jnp.zeros_like(core), (me % ROW < 1).astype(core.dtype), (me % ROW < 2).astype(core.dtype)]
    ).astype(jnp.int32)

    def own(g, at):
        return (0, group_of(at[0], g))

    def halo(row, lane):
        return lambda g, at: (row, lane + g)

    grad_q, other_q, part = pl.pallas_call(
        attend,
        grid_spec=pltpu.PrefetchScalarGridSpec(
            num_scalar_prefetch=1,
            grid=(2,),
            in_specs=[
                pl.BlockSpec((1, tok), lambda g, at: (0, 0)),
                pl.BlockSpec((tok, WIDE), own),
                pl.BlockSpec((tok, WIDE), own),
                pl.BlockSpec((tok, WIDE), halo(0, 0)),
                pl.BlockSpec((tok, WIDE), halo(1, 0)),
                pl.BlockSpec((tok, DH), own),
                pl.BlockSpec((tok, DH), own),
                pl.BlockSpec((tok, DH), halo(0, 0)),
                pl.BlockSpec((tok, DH), halo(0, 2)),
                pl.BlockSpec((tok, DH), halo(0, 0)),
                pl.BlockSpec((tok, DH), halo(0, 2)),
                pl.BlockSpec((ID_ROWS, tok), lambda g, at: (tok // ID_ROWS, 0)),
                pl.BlockSpec((ID_ROWS, tok), lambda g, at: (tok // ID_ROWS, 0)),
            ],
            out_specs=(
                pl.BlockSpec((tok, WIDE), own),
                pl.BlockSpec((tok, WIDE), halo(0, 0)),
                pl.BlockSpec((4, 3 * tok, DH), lambda g, at: (0, 0, 0)),
            ),
        ),
        out_shape=(
            jax.ShapeDtypeStruct(q.shape, jnp.bfloat16),
            jax.ShapeDtypeStruct((tok, 2 * WIDE), jnp.bfloat16),
            jax.ShapeDtypeStruct((4, 3 * tok, DH), jnp.bfloat16),
        ),
        compiler_params=pltpu.CompilerParams(vmem_limit_bytes=24 * 1024 * 1024),
        name="attend",
    )(place, segment_ids.reshape(1, tok), q, c, swapped, swapped, keys, values, one, one, two, two, one, two)
    total = sum(to_owner(part[step], step).astype(jnp.float32) for step in range(4))
    back_one = shifted(total[tok : 2 * tok].astype(jnp.bfloat16), -1)
    back_two = shifted(total[2 * tok :].astype(jnp.bfloat16), -2)
    back_q = other_core(other_q)
    outer = jnp.concatenate([back_q[:, :WIDE], grad_q[:, WIDE : 3 * WIDE], back_q[:, WIDE:]], 1)
    inner = jnp.concatenate([grad_q[:, :WIDE], back_q, grad_q[:, 3 * WIDE :]], 1)
    grad_q = jnp.where(core == 0, inner, outer)
    grad_k, grad_v = pl.pallas_call(
        finish,
        out_shape=(jax.ShapeDtypeStruct((DH // 2, tok), jnp.float32),) * 2,
        name="finish",
    )(total[:tok], back_one, back_two)
    return (grad_q[None], grad_k.T, grad_v.T)


def solution(mesh):
    placed = (
        P("section", "ctx", None),
        P("ctx", None),
        P("ctx", None),
        P("section", "ctx", None),
        P("ctx"),
    )
    return jax.shard_map(
        on_device,
        mesh=mesh,
        in_specs=placed,
        out_specs=(P("section", "ctx", None), P("ctx", "section"), P("ctx", "section")),
        check_vma=False,
    )
```

```python
import jax
import jax.numpy as jnp
from jax import lax
from jax.experimental import pallas as pl
from jax.experimental.pallas import tpu as pltpu
from jax.sharding import PartitionSpec as P

DH = 128
TOK = 128
RATIO = 5
WIDE = RATIO * DH
ROW = 4
ID_ROWS = 16
SCALE = DH ** (-0.5)
LOG2E = 1.4426950408889634
NEG = -1e30
AXES = ("section", "ctx")
NT = (((1,), (1,)), ((), ()))
TN = (((0,), (0,)), ((), ()))


def permuted(x, target):
    sections, cycle = lax.axis_size("section"), lax.axis_size("ctx")
    found = []
    for s in range(sections):
        for c in range(cycle):
            to = target(s, c)
            if 0 <= to[1] < cycle:
                found.append((s * cycle + c, to[0] * cycle + to[1]))
    return lax.ppermute(x, AXES, found)


def fetched(x):
    def target(s, c):
        to = c + 1 + s // 2 % 2
        return (s ^ 4 if c // ROW != to // ROW else s, to)

    return permuted(x, target)


def returned(x):
    def target(s, c):
        to = c - 1 - s % 2
        return ((3 - s // 2) * 2 + s % 2 if c // ROW != to // ROW else s, to)

    return permuted(x, target)


def next_chip(x):
    return permuted(x, lambda s, c: (s ^ 2, c))


def other_core(x):
    return permuted(x, lambda s, c: (s ^ 1, c))


def group_of(core, slot):
    return core + slot * (3 - 2 * core)


def to_owner(x, step):
    def target(s, c):
        share = (s // 2) ^ step
        return (group_of(s % 2, share // 2) * 2 + share % 2, c)

    return permuted(x, target)


def pack_halo(place_ref, ids_ref, k_ref, v_ref, out_ref):
    out_ref[:TOK, :DH] = k_ref[...]
    out_ref[:TOK, DH:] = v_ref[...]
    ids = jnp.broadcast_to((ids_ref[...] + 1).astype(jnp.float32), (ID_ROWS, TOK)).astype(jnp.bfloat16)
    out_ref[TOK:, :DH] = ids
    out_ref[TOK:, DH:] = ids


def pack_rows(place_ref, q_ref, c_ref, q_out_ref, c_out_ref):
    q_out_ref[...] = q_ref[...]
    c_out_ref[...] = c_ref[...]


def attend(
    place_ref, ids_ref, q_ref, c_ref, oq_ref, oc_ref, k_ref, v_ref, fetched_ref, swapped_ref, dq_ref, odq_ref, part_ref
):
    slot = pl.program_id(0)
    ids = ids_ref[...].astype(jnp.float32)
    first = ids[:, 0:1]
    even = place_ref[1] % 2 == 0
    one = jnp.where(even, fetched_ref[...], swapped_ref[...])
    two = jnp.where(even, swapped_ref[...], fetched_ref[...])
    keys = jnp.concatenate([k_ref[...], one[:TOK, :DH], two[:TOK, :DH]], 0)
    values = jnp.concatenate([v_ref[...], one[:TOK, DH:], two[:TOK, DH:]], 0)
    row = lax.broadcasted_iota(jnp.int32, (TOK, TOK), 0)
    col = lax.broadcasted_iota(jnp.int32, (TOK, TOK), 1)
    wide = jnp.broadcast_to(ids, (TOK, TOK))
    biases = [jnp.where((wide.T == wide) & (row <= col), 0.0, NEG)]
    for halo in (one, two):
        before = halo[TOK:, :DH].astype(jnp.float32)[0:1]
        held = jnp.sum(jnp.where(before == first + 1.0, 1.0, 0.0), -1, keepdims=True)
        biases.append(jnp.where((wide == first) & (row.astype(jnp.float32) >= TOK - held), 0.0, NEG))
    bias = jnp.concatenate(biases, 0)
    grad_k = jnp.zeros((3 * TOK, DH), jnp.float32)
    grad_v = jnp.zeros((3 * TOK, DH), jnp.float32)
    for layer_q, layer_c, out in ((q_ref, c_ref, dq_ref), (oq_ref, oc_ref, odq_ref)):
        queries = jnp.concatenate([layer_q[:, h * DH : (h + 1) * DH] for h in range(RATIO)], 0)
        cots = jnp.concatenate([layer_c[:, h * DH : (h + 1) * DH] for h in range(RATIO)], 0)
        scores = lax.dot_general(keys, queries, NT, preferred_element_type=jnp.float32)
        grad_probs = lax.dot_general(values, cots, NT, preferred_element_type=jnp.float32)
        probs_low, scaled_low = [], []
        for h in range(RATIO):
            at = slice(h * TOK, (h + 1) * TOK)
            s = scores[:, at] * (SCALE * LOG2E) + bias
            e = jnp.exp2(s - jnp.max(s, 0, keepdims=True))
            p = e * (1.0 / jnp.sum(e, 0, keepdims=True))
            low = p.astype(jnp.bfloat16)
            g = grad_probs[:, at]
            dot = jnp.sum(low.astype(jnp.float32) * g, 0, keepdims=True)
            probs_low.append(low)
            scaled_low.append((p * (g - dot) * SCALE).astype(jnp.bfloat16))
        probs_low = jnp.concatenate(probs_low, 1)
        scaled_low = jnp.concatenate(scaled_low, 1)
        grad_v += jnp.dot(probs_low, cots, preferred_element_type=jnp.float32)
        grad_k += jnp.dot(scaled_low, queries, preferred_element_type=jnp.float32)
        grad_q = lax.dot_general(keys, scaled_low, TN, preferred_element_type=jnp.float32)
        for h in range(RATIO):
            at = slice(h * TOK, (h + 1) * TOK)
            out[:, at] = grad_q[:, at].T.astype(jnp.bfloat16)
    half = DH // 2
    grad_k = grad_k.astype(jnp.bfloat16)
    grad_v = grad_v.astype(jnp.bfloat16)
    shares = (
        jnp.concatenate([grad_k[:, :half], grad_v[:, :half]], 1),
        jnp.concatenate([grad_k[:, half:], grad_v[:, half:]], 1),
    )
    for side in range(2):
        part_ref[(2 * slot + side) ^ place_ref[1], :TOK, :] = shares[side][:TOK]
        for block in (1, 2):
            carrier = 2 * (slot ^ place_ref[1 + block]) + block - 1
            rows = slice((1 + side) * TOK, (2 + side) * TOK)
            part_ref[carrier ^ place_ref[1], rows, :] = shares[side][block * TOK : (block + 1) * TOK]


def finish(place_ref, own_ref, back_ref, swapped_ref, dq_ref, dk_ref, dv_ref):
    mine = back_ref[pl.ds(pl.multiple_of(place_ref[0] * TOK, TOK), TOK), :]
    total = own_ref[...] + mine.astype(jnp.float32) + swapped_ref[...].astype(jnp.float32)
    total = total.T
    dk_ref[...] = total[: DH // 2]
    dv_ref[...] = total[DH // 2 :]


def on_device(queries, keys, values, cotangent, segment_ids):
    section, me = lax.axis_index("section"), lax.axis_index("ctx")
    core, y_lo = section % 2, section // 2
    tok = keys.shape[0]
    q, c = queries[0], cotangent[0]

    ids = segment_ids.reshape(1, tok)
    place = jnp.stack([core, y_lo, (me % ROW < 1).astype(core.dtype), (me % ROW < 2).astype(core.dtype)])
    place = place.astype(jnp.int32)

    def own(g, at):
        return (0, group_of(at[0], g))

    def others(g, at):
        return (0, group_of(1 - at[0], g))

    def column(g, at):
        return (0, g)

    def fixed(g, at):
        return (0, 0)

    sent = pl.pallas_call(
        pack_halo,
        grid_spec=pltpu.PrefetchScalarGridSpec(
            num_scalar_prefetch=1,
            grid=(2,),
            in_specs=[pl.BlockSpec((1, tok), fixed), pl.BlockSpec((tok, DH), own), pl.BlockSpec((tok, DH), own)],
            out_specs=pl.BlockSpec((tok + ID_ROWS, 2 * DH), column),
        ),
        out_shape=jax.ShapeDtypeStruct((tok + ID_ROWS, 4 * DH), jnp.bfloat16),
        name="pack_halo",
    )(place, ids, keys, values)
    halo = fetched(sent)
    halo_other = next_chip(halo)
    q, c, _ = lax.optimization_barrier((q, c, sent))
    other_rows = pl.pallas_call(
        pack_rows,
        grid_spec=pltpu.PrefetchScalarGridSpec(
            num_scalar_prefetch=1,
            grid=(2,),
            in_specs=[pl.BlockSpec((tok, WIDE), others), pl.BlockSpec((tok, WIDE), others)],
            out_specs=(pl.BlockSpec((tok, WIDE), column),) * 2,
        ),
        out_shape=(jax.ShapeDtypeStruct((tok, 2 * WIDE), jnp.bfloat16),) * 2,
        name="pack_rows",
    )(place, q, c)
    other_rows = [other_core(x) for x in other_rows]
    grad_q, other_q, part = pl.pallas_call(
        attend,
        grid_spec=pltpu.PrefetchScalarGridSpec(
            num_scalar_prefetch=1,
            grid=(2,),
            in_specs=[
                pl.BlockSpec((1, tok), fixed),
                pl.BlockSpec((tok, WIDE), own),
                pl.BlockSpec((tok, WIDE), own),
                pl.BlockSpec((tok, WIDE), column),
                pl.BlockSpec((tok, WIDE), column),
                pl.BlockSpec((tok, DH), own),
                pl.BlockSpec((tok, DH), own),
                pl.BlockSpec((tok + ID_ROWS, 2 * DH), column),
                pl.BlockSpec((tok + ID_ROWS, 2 * DH), column),
            ],
            out_specs=(
                pl.BlockSpec((tok, WIDE), own),
                pl.BlockSpec((tok, WIDE), column),
                pl.BlockSpec((4, 3 * tok, DH), lambda g, at: (0, 0, 0)),
            ),
        ),
        out_shape=(
            jax.ShapeDtypeStruct(q.shape, jnp.bfloat16),
            jax.ShapeDtypeStruct((tok, 2 * WIDE), jnp.bfloat16),
            jax.ShapeDtypeStruct((4, 3 * tok, DH), jnp.bfloat16),
        ),
        compiler_params=pltpu.CompilerParams(vmem_limit_bytes=24 * 1024 * 1024),
        name="attend",
    )(place, ids, q, c, *other_rows, keys, values, halo, halo_other)
    shares = [to_owner(part[step], step) for step in range(4)]
    total = sum(share[:tok].astype(jnp.float32) for share in shares)
    back = sum(share[tok:].astype(jnp.float32) for share in shares).astype(jnp.bfloat16)
    back = returned(back)
    back_other = other_core(jnp.where(core == 0, back[tok:], back[:tok]))
    back_q = other_core(other_q)
    outer = jnp.concatenate([back_q[:, :WIDE], grad_q[:, WIDE : 3 * WIDE], back_q[:, WIDE:]], 1)
    inner = jnp.concatenate([grad_q[:, :WIDE], back_q, grad_q[:, 3 * WIDE :]], 1)
    grad_q = jnp.where(core == 0, inner, outer)
    vmem = pl.BlockSpec(memory_space=pltpu.VMEM)
    grad_k, grad_v = pl.pallas_call(
        finish,
        in_specs=[pl.BlockSpec(memory_space=pltpu.SMEM), vmem, vmem, vmem, pl.BlockSpec(memory_space=pl.ANY)],
        out_shape=(jax.ShapeDtypeStruct((DH // 2, tok), jnp.float32),) * 2,
        name="finish",
    )(place, total, back, back_other, grad_q)
    return (grad_q[None], grad_k.T, grad_v.T)


def solution(mesh):
    placed = (
        P("section", "ctx", None),
        P("ctx", None),
        P("ctx", None),
        P("section", "ctx", None),
        P("ctx"),
    )
    return jax.shard_map(
        on_device,
        mesh=mesh,
        in_specs=placed,
        out_specs=(P("section", "ctx", None), P("ctx", "section"), P("ctx", "section")),
        check_vma=False,
    )
```

```python
import jax
import jax.numpy as jnp
from jax import lax
from jax.experimental import pallas as pl
from jax.experimental.pallas import tpu as pltpu
from jax.sharding import PartitionSpec as P

DH = 128
TOK = 128
RATIO = 5
WIDE = RATIO * DH
ROW = 4
ID_ROWS = 16
SCALE = DH ** (-0.5)
LOG2E = 1.4426950408889634
NEG = -1e30
OWN_FLOPS = 1 << 34
AXES = ("section", "ctx")
NT = (((1,), (1,)), ((), ()))
TN = (((0,), (0,)), ((), ()))


def permuted(x, target):
    sections, cycle = lax.axis_size("section"), lax.axis_size("ctx")
    found = []
    for s in range(sections):
        for c in range(cycle):
            to = target(s, c)
            if 0 <= to[1] < cycle:
                found.append((s * cycle + c, to[0] * cycle + to[1]))
    return lax.ppermute(x, AXES, found)


def shifted(x, by):
    def target(s, c):
        leaves = c // ROW != (c + by) // ROW
        return ((3 - s // 2) * 2 + s % 2 if leaves else s, c + by)

    return permuted(x, target)


def returned(x):
    def target(s, c):
        to = c - 1 - s % 2
        return ((3 - s // 2) * 2 + s % 2 if c // ROW != to // ROW else s, to)

    return permuted(x, target)


def other_core(x):
    return permuted(x, lambda s, c: (s ^ 1, c))


def group_of(core, slot):
    return core + slot * (3 - 2 * core)


def to_owner(x, step):
    def target(s, c):
        share = (s // 2) ^ step
        return (group_of(s % 2, share // 2) * 2 + share % 2, c)

    return permuted(x, target)


def core_groups(core):
    return [group_of(core, slot) for slot in range(2)]


def columns(group, width):
    return pl.ds(pl.multiple_of(group * width, width), width)


def run(copies):
    for copy in copies:
        copy.start()
    for copy in copies:
        copy.wait()


def pack_halo(ids_ref, k_ref, v_ref, out_ref, ids_vmem, sems):
    copies = [pltpu.make_async_copy(ids_ref, ids_vmem, sems.at[4])]
    for slot, group in enumerate(core_groups(lax.axis_index("section") % 2)):
        for i, ref in enumerate((k_ref, v_ref)):
            to = out_ref.at[pl.ds(0, TOK), pl.ds((2 * slot + i) * DH, DH)]
            copies.append(pltpu.make_async_copy(ref.at[:, columns(group, DH)], to, sems.at[2 * slot + i]))
    run(copies)
    ids = jnp.broadcast_to((ids_vmem[...] + 1).astype(jnp.float32), (ID_ROWS, TOK)).astype(jnp.bfloat16)
    for column in range(4):
        out_ref[TOK:, column * DH : (column + 1) * DH] = ids


def pack_rows(q_ref, c_ref, out_ref, sems):
    copies = []
    for slot, group in enumerate(core_groups(1 - lax.axis_index("section") % 2)):
        for i, ref in enumerate((q_ref, c_ref)):
            to = out_ref.at[pl.ds(i * TOK, TOK), pl.ds(slot * WIDE, WIDE)]
            copies.append(pltpu.make_async_copy(ref.at[:, columns(group, WIDE)], to, sems.at[2 * slot + i]))
    run(copies)


def one_layer(ids_ref, q_ref, c_ref, k_ref, v_ref, one_ref, two_ref, dq_ref):
    ids = ids_ref[...].astype(jnp.float32)
    first = ids[:, 0:1]
    keys = jnp.concatenate([k_ref[...], one_ref[:TOK, :DH], two_ref[:TOK, :DH]], 0)
    values = jnp.concatenate([v_ref[...], one_ref[:TOK, DH:], two_ref[:TOK, DH:]], 0)
    row = lax.broadcasted_iota(jnp.int32, (TOK, TOK), 0)
    col = lax.broadcasted_iota(jnp.int32, (TOK, TOK), 1)
    wide = jnp.broadcast_to(ids, (TOK, TOK))
    biases = [jnp.where((wide.T == wide) & (row <= col), 0.0, NEG)]
    for halo in (one_ref, two_ref):
        before = halo[TOK:, :DH].astype(jnp.float32)[0:1]
        held = jnp.sum(jnp.where(before == first + 1.0, 1.0, 0.0), -1, keepdims=True)
        biases.append(jnp.where((wide == first) & (row.astype(jnp.float32) >= TOK - held), 0.0, NEG))
    bias = jnp.concatenate(biases, 0)
    queries = jnp.concatenate([q_ref[:, h * DH : (h + 1) * DH] for h in range(RATIO)], 0)
    cots = jnp.concatenate([c_ref[:, h * DH : (h + 1) * DH] for h in range(RATIO)], 0)
    scores = lax.dot_general(keys, queries, NT, preferred_element_type=jnp.float32)
    grad_probs = lax.dot_general(values, cots, NT, preferred_element_type=jnp.float32)
    probs_low, scaled_low = [], []
    for h in range(RATIO):
        at = slice(h * TOK, (h + 1) * TOK)
        s = scores[:, at] * (SCALE * LOG2E) + bias
        e = jnp.exp2(s - jnp.max(s, 0, keepdims=True))
        p = e * (1.0 / jnp.sum(e, 0, keepdims=True))
        low = p.astype(jnp.bfloat16)
        g = grad_probs[:, at]
        dot = jnp.sum(low.astype(jnp.float32) * g, 0, keepdims=True)
        probs_low.append(low)
        scaled_low.append((p * (g - dot) * SCALE).astype(jnp.bfloat16))
    probs_low = jnp.concatenate(probs_low, 1)
    scaled_low = jnp.concatenate(scaled_low, 1)
    grad_v = jnp.dot(probs_low, cots, preferred_element_type=jnp.float32)
    grad_k = jnp.dot(scaled_low, queries, preferred_element_type=jnp.float32)
    grad_q = lax.dot_general(keys, scaled_low, TN, preferred_element_type=jnp.float32)
    for h in range(RATIO):
        at = slice(h * TOK, (h + 1) * TOK)
        dq_ref[:, at] = grad_q[:, at].T.astype(jnp.bfloat16)
    return grad_k, grad_v


def attend_own(place_ref, ids_ref, q_ref, c_ref, k_ref, v_ref, one_ref, two_ref, dq_ref, dk_ref, dv_ref):
    grad_k, grad_v = one_layer(ids_ref, q_ref, c_ref, k_ref, v_ref, one_ref, two_ref, dq_ref)
    dk_ref[...] = grad_k
    dv_ref[...] = grad_v


def attend_other(
    place_ref, ids_ref, q_ref, c_ref, k_ref, v_ref, one_ref, two_ref, dk_ref, dv_ref, dq_ref, part_ref
):
    slot = pl.program_id(0)
    grad_k, grad_v = one_layer(ids_ref, q_ref, c_ref, k_ref, v_ref, one_ref, two_ref, dq_ref)
    half = DH // 2
    grad_k = (grad_k + dk_ref[...]).astype(jnp.bfloat16)
    grad_v = (grad_v + dv_ref[...]).astype(jnp.bfloat16)
    shares = (
        jnp.concatenate([grad_k[:, :half], grad_v[:, :half]], 1),
        jnp.concatenate([grad_k[:, half:], grad_v[:, half:]], 1),
    )
    for side in range(2):
        part_ref[(2 * slot + side) ^ place_ref[1], :TOK, :] = shares[side][:TOK]
        for block in (1, 2):
            carrier = 2 * (slot ^ place_ref[1 + block]) + block - 1
            rows = slice((1 + side) * TOK, (2 + side) * TOK)
            part_ref[carrier ^ place_ref[1], rows, :] = shares[side][block * TOK : (block + 1) * TOK]


def finish(own_ref, back_ref, swapped_ref, dq_in_ref, dq_ref, dk_ref, dv_ref, total_ref, sems):
    core = lax.axis_index("section") % 2
    half = DH // 2
    copies = []
    for slot, group in enumerate(core_groups(1 - core)):
        src = swapped_ref.at[:, pl.ds(slot * WIDE, WIDE)]
        copies.append(pltpu.make_async_copy(src, dq_ref.at[:, columns(group, WIDE)], sems.at[slot]))
    for copy in copies:
        copy.start()
    mine = back_ref[pl.ds(pl.multiple_of(core * TOK, TOK), TOK), :]
    total = own_ref[...] + mine.astype(jnp.float32) + swapped_ref[:, 2 * WIDE :].astype(jnp.float32)
    total_ref[...] = total.T
    for i, ref in enumerate((dk_ref, dv_ref)):
        copies.append(pltpu.make_async_copy(total_ref.at[pl.ds(i * half, half)], ref, sems.at[2 + i]))
        copies[-1].start()
    for copy in copies:
        copy.wait()


def on_device(queries, keys, values, cotangent, segment_ids):
    section, me = lax.axis_index("section"), lax.axis_index("ctx")
    core, y_lo = section % 2, section // 2
    tok = keys.shape[0]
    q, c = queries[0], cotangent[0]
    ids = segment_ids.reshape(1, tok)
    hbm = pl.BlockSpec(memory_space=pltpu.HBM)
    vmem = pl.BlockSpec(memory_space=pltpu.VMEM)

    def own(g, at):
        return (0, group_of(at[0], g))

    def column(g, at):
        return (0, g)

    def fixed(g, at):
        return (0, 0)

    sent = pl.pallas_call(
        pack_halo,
        in_specs=[hbm] * 3,
        out_specs=vmem,
        out_shape=jax.ShapeDtypeStruct((tok + ID_ROWS, 4 * DH), jnp.bfloat16),
        scratch_shapes=[pltpu.VMEM((1, tok), jnp.int32), pltpu.SemaphoreType.DMA((5,))],
        compiler_params=pltpu.CompilerParams(vmem_limit_bytes=8 * 1024 * 1024),
        name="pack_halo",
    )(*(pltpu.with_memory_space_constraint(x, pltpu.HBM) for x in (ids, keys, values)))
    one, two = shifted(sent, 1), shifted(sent, 2)
    q, c, _ = lax.optimization_barrier((q, c, sent))
    rows = pl.pallas_call(
        pack_rows,
        in_specs=[hbm] * 2,
        out_specs=vmem,
        out_shape=jax.ShapeDtypeStruct((2 * tok, 2 * WIDE), jnp.bfloat16),
        scratch_shapes=[pltpu.SemaphoreType.DMA((4,))],
        compiler_params=pltpu.CompilerParams(vmem_limit_bytes=8 * 1024 * 1024),
        name="pack_rows",
    )(*(pltpu.with_memory_space_constraint(x, pltpu.HBM) for x in (q, c)))
    rows = other_core(rows)
    place = jnp.stack([core, y_lo, (me % ROW < 1).astype(core.dtype), (me % ROW < 2).astype(core.dtype)])
    place = place.astype(jnp.int32)
    shared = [
        pl.BlockSpec((tok, DH), own),
        pl.BlockSpec((tok, DH), own),
        pl.BlockSpec((tok + ID_ROWS, 2 * DH), column),
        pl.BlockSpec((tok + ID_ROWS, 2 * DH), column),
    ]
    grads = (pl.BlockSpec((3 * tok, DH), column),) * 2
    params = pltpu.CompilerParams(vmem_limit_bytes=24 * 1024 * 1024)
    grad_q, grad_k, grad_v = pl.pallas_call(
        attend_own,
        grid_spec=pltpu.PrefetchScalarGridSpec(
            num_scalar_prefetch=1,
            grid=(2,),
            in_specs=[
                pl.BlockSpec((1, tok), fixed),
                pl.BlockSpec((tok, WIDE), own),
                pl.BlockSpec((tok, WIDE), own),
                *shared,
            ],
            out_specs=(pl.BlockSpec((tok, WIDE), own), *grads),
        ),
        out_shape=(
            jax.ShapeDtypeStruct(q.shape, jnp.bfloat16),
            jax.ShapeDtypeStruct((3 * tok, 2 * DH), jnp.float32),
            jax.ShapeDtypeStruct((3 * tok, 2 * DH), jnp.float32),
        ),
        compiler_params=params,
        cost_estimate=pl.CostEstimate(flops=OWN_FLOPS, bytes_accessed=0, transcendentals=0),
        name="attend_own",
    )(place, ids, q, c, keys, values, one, two)
    other_q, part = pl.pallas_call(
        attend_other,
        grid_spec=pltpu.PrefetchScalarGridSpec(
            num_scalar_prefetch=1,
            grid=(2,),
            in_specs=[
                pl.BlockSpec((1, tok), fixed),
                pl.BlockSpec((tok, WIDE), column),
                pl.BlockSpec((tok, WIDE), lambda g, at: (1, g)),
                *shared,
                *grads,
            ],
            out_specs=(pl.BlockSpec((tok, WIDE), column), pl.BlockSpec((4, 3 * tok, DH), lambda g, at: (0, 0, 0))),
        ),
        out_shape=(
            jax.ShapeDtypeStruct((tok, 2 * WIDE), jnp.bfloat16),
            jax.ShapeDtypeStruct((4, 3 * tok, DH), jnp.bfloat16),
        ),
        compiler_params=params,
        name="attend_other",
    )(place, ids, rows, rows, keys, values, one, two, grad_k, grad_v)
    shares = [to_owner(part[step], step) for step in range(4)]
    total = sum(share[:tok].astype(jnp.float32) for share in shares)
    back = sum(share[tok:].astype(jnp.float32) for share in shares).astype(jnp.bfloat16)
    back = returned(back)
    swapped = other_core(jnp.concatenate([other_q, jnp.where(core == 0, back[tok:], back[:tok])], 1))
    grad_q, grad_k, grad_v = pl.pallas_call(
        finish,
        in_specs=[vmem, vmem, vmem, hbm],
        out_specs=(hbm, hbm, hbm),
        out_shape=(
            jax.ShapeDtypeStruct(q.shape, jnp.bfloat16),
            jax.ShapeDtypeStruct((DH // 2, tok), jnp.float32),
            jax.ShapeDtypeStruct((DH // 2, tok), jnp.float32),
        ),
        scratch_shapes=[pltpu.VMEM((DH, tok), jnp.float32), pltpu.SemaphoreType.DMA((4,))],
        input_output_aliases={3: 0},
        name="finish",
    )(total, back, swapped, grad_q)
    return (grad_q[None], grad_k.T, grad_v.T)


def solution(mesh):
    placed = (
        P("section", "ctx", None),
        P("ctx", None),
        P("ctx", None),
        P("section", "ctx", None),
        P("ctx"),
    )
    return jax.shard_map(
        on_device,
        mesh=mesh,
        in_specs=placed,
        out_specs=(P("section", "ctx", None), P("ctx", "section"), P("ctx", "section")),
        check_vma=False,
    )
```

```python
import jax
import jax.numpy as jnp
from jax import lax
from jax.experimental import pallas as pl
from jax.experimental.pallas import tpu as pltpu
from jax.sharding import PartitionSpec as P

DH = 128
TOK = 128
RATIO = 5
WIDE = RATIO * DH
ROW = 4
ID_ROWS = 16
SCALE = DH ** (-0.5)
LOG2E = 1.4426950408889634
NEG = -1e30
MASK_FLOPS = 1 << 34
AXES = ("section", "ctx")
NT = (((1,), (1,)), ((), ()))
TN = (((0,), (0,)), ((), ()))


def permuted(x, target):
    sections, cycle = lax.axis_size("section"), lax.axis_size("ctx")
    found = []
    for s in range(sections):
        for c in range(cycle):
            to = target(s, c)
            if 0 <= to[1] < cycle:
                found.append((s * cycle + c, to[0] * cycle + to[1]))
    return lax.ppermute(x, AXES, found)


def shifted(x, by):
    def target(s, c):
        leaves = c // ROW != (c + by) // ROW
        return ((3 - s // 2) * 2 + s % 2 if leaves else s, c + by)

    return permuted(x, target)


def returned(x):
    def target(s, c):
        to = c - 1 - s % 2
        return ((3 - s // 2) * 2 + s % 2 if c // ROW != to // ROW else s, to)

    return permuted(x, target)


def other_core(x):
    return permuted(x, lambda s, c: (s ^ 1, c))


def group_of(core, slot):
    return core + slot * (3 - 2 * core)


def to_owner(x, step):
    def target(s, c):
        share = (s // 2) ^ step
        return (group_of(s % 2, share // 2) * 2 + share % 2, c)

    return permuted(x, target)


def core_groups(core):
    return [group_of(core, slot) for slot in range(2)]


def columns(group, width):
    return pl.ds(pl.multiple_of(group * width, width), width)


def run(copies):
    for copy in copies:
        copy.start()
    for copy in copies:
        copy.wait()


def pack_halo(ids_ref, k_ref, v_ref, out_ref, ids_vmem, sems):
    copies = [pltpu.make_async_copy(ids_ref, ids_vmem, sems.at[4])]
    for slot, group in enumerate(core_groups(lax.axis_index("section") % 2)):
        for i, ref in enumerate((k_ref, v_ref)):
            to = out_ref.at[pl.ds(0, TOK), pl.ds((2 * slot + i) * DH, DH)]
            copies.append(pltpu.make_async_copy(ref.at[:, columns(group, DH)], to, sems.at[2 * slot + i]))
    run(copies)
    ids = jnp.broadcast_to((ids_vmem[...] + 1).astype(jnp.float32), (ID_ROWS, TOK)).astype(jnp.bfloat16)
    for column in range(4):
        out_ref[TOK:, column * DH : (column + 1) * DH] = ids


def pack_rows(q_ref, c_ref, out_ref, sems):
    copies = []
    for slot, group in enumerate(core_groups(1 - lax.axis_index("section") % 2)):
        for i, ref in enumerate((q_ref, c_ref)):
            to = out_ref.at[pl.ds(i * TOK, TOK), pl.ds(slot * WIDE, WIDE)]
            copies.append(pltpu.make_async_copy(ref.at[:, columns(group, WIDE)], to, sems.at[2 * slot + i]))
    run(copies)


def mask(ids_ref, one_ref, two_ref, out_ref):
    ids = ids_ref[...].astype(jnp.float32)
    first = ids[:, 0:1]
    row = lax.broadcasted_iota(jnp.int32, (TOK, TOK), 0)
    col = lax.broadcasted_iota(jnp.int32, (TOK, TOK), 1)
    wide = jnp.broadcast_to(ids, (TOK, TOK))
    out_ref[:TOK] = jnp.where((wide.T == wide) & (row <= col), 0.0, NEG)
    for block, halo in enumerate((one_ref, two_ref)):
        before = halo[TOK:, :DH].astype(jnp.float32)[0:1]
        held = jnp.sum(jnp.where(before == first + 1.0, 1.0, 0.0), -1, keepdims=True)
        out_ref[(block + 1) * TOK : (block + 2) * TOK] = jnp.where(
            (wide == first) & (row.astype(jnp.float32) >= TOK - held), 0.0, NEG
        )


def attend(place_ref, bias_ref, q_ref, c_ref, oqc_ref, k_ref, v_ref, one_ref, two_ref, dq_ref, odq_ref, part_ref):
    slot = pl.program_id(0)
    group = group_of(place_ref[0], slot)

    def lanes(start, size=DH):
        return pl.ds(pl.multiple_of(start, DH), size)

    keys = jnp.concatenate(
        [k_ref[:, lanes(group * DH)], one_ref[:TOK, lanes(slot * 2 * DH)], two_ref[:TOK, lanes(slot * 2 * DH)]], 0
    )
    values = jnp.concatenate(
        [v_ref[:, lanes(group * DH)], one_ref[:TOK, lanes((slot * 2 + 1) * DH)], two_ref[:TOK, lanes((slot * 2 + 1) * DH)]],
        0,
    )
    bias = bias_ref[...]
    grad_k = jnp.zeros((3 * TOK, DH), jnp.float32)
    grad_v = jnp.zeros((3 * TOK, DH), jnp.float32)
    for mine in (True, False):
        start = (group if mine else slot) * WIDE
        queries, cots = [], []
        for h in range(RATIO):
            at = lanes(start + h * DH)
            queries.append(q_ref[:, at] if mine else oqc_ref[:TOK, at])
            cots.append(c_ref[:, at] if mine else oqc_ref[TOK:, at])
        queries, cots = jnp.concatenate(queries, 0), jnp.concatenate(cots, 0)
        scores = lax.dot_general(keys, queries, NT, preferred_element_type=jnp.float32)
        grad_probs = lax.dot_general(values, cots, NT, preferred_element_type=jnp.float32)
        probs_low, scaled_low = [], []
        for h in range(RATIO):
            at = slice(h * TOK, (h + 1) * TOK)
            s = scores[:, at] * (SCALE * LOG2E) + bias
            e = jnp.exp2(s - jnp.max(s, 0, keepdims=True))
            p = e * (1.0 / jnp.sum(e, 0, keepdims=True))
            low = p.astype(jnp.bfloat16)
            g = grad_probs[:, at]
            dot = jnp.sum(low.astype(jnp.float32) * g, 0, keepdims=True)
            probs_low.append(low)
            scaled_low.append((p * (g - dot) * SCALE).astype(jnp.bfloat16))
        probs_low = jnp.concatenate(probs_low, 1)
        scaled_low = jnp.concatenate(scaled_low, 1)
        grad_v += jnp.dot(probs_low, cots, preferred_element_type=jnp.float32)
        grad_k += jnp.dot(scaled_low, queries, preferred_element_type=jnp.float32)
        grad_q = lax.dot_general(keys, scaled_low, TN, preferred_element_type=jnp.float32)
        out = dq_ref if mine else odq_ref
        for h in range(RATIO):
            out[:, lanes(slot * WIDE + h * DH)] = grad_q[:, h * TOK : (h + 1) * TOK].T.astype(jnp.bfloat16)
    half = DH // 2
    grad_k = grad_k.astype(jnp.bfloat16)
    grad_v = grad_v.astype(jnp.bfloat16)
    shares = (
        jnp.concatenate([grad_k[:, :half], grad_v[:, :half]], 1),
        jnp.concatenate([grad_k[:, half:], grad_v[:, half:]], 1),
    )
    for side in range(2):
        part_ref[(2 * slot + side) ^ place_ref[1], :TOK, :] = shares[side][:TOK]
        for block in (1, 2):
            carrier = 2 * (slot ^ place_ref[1 + block]) + block - 1
            rows = slice((1 + side) * TOK, (2 + side) * TOK)
            part_ref[carrier ^ place_ref[1], rows, :] = shares[side][block * TOK : (block + 1) * TOK]


def finish(own_ref, back_ref, swapped_ref, own_q_ref, dq_ref, dk_ref, dv_ref, total_ref, sems):
    core = lax.axis_index("section") % 2
    half = DH // 2
    copies = []
    for i, ref in enumerate((own_q_ref, swapped_ref)):
        for slot, group in enumerate(core_groups(core if i == 0 else 1 - core)):
            src = ref.at[:, pl.ds(slot * WIDE, WIDE)]
            copies.append(pltpu.make_async_copy(src, dq_ref.at[:, columns(group, WIDE)], sems.at[2 * i + slot]))
    for copy in copies:
        copy.start()
    mine = back_ref[pl.ds(pl.multiple_of(core * TOK, TOK), TOK), :]
    total = own_ref[...] + mine.astype(jnp.float32) + swapped_ref[:, 2 * WIDE :].astype(jnp.float32)
    total_ref[...] = total.T
    for i, ref in enumerate((dk_ref, dv_ref)):
        copies.append(pltpu.make_async_copy(total_ref.at[pl.ds(i * half, half)], ref, sems.at[4 + i]))
        copies[-1].start()
    for copy in copies:
        copy.wait()


def on_device(queries, keys, values, cotangent, segment_ids):
    section, me = lax.axis_index("section"), lax.axis_index("ctx")
    core, y_lo = section % 2, section // 2
    tok = keys.shape[0]
    q, c = queries[0], cotangent[0]
    ids = segment_ids.reshape(1, tok)
    hbm = pl.BlockSpec(memory_space=pltpu.HBM)
    vmem = pl.BlockSpec(memory_space=pltpu.VMEM)

    small = pltpu.CompilerParams(vmem_limit_bytes=4 * 1024 * 1024)

    sent = pl.pallas_call(
        pack_halo,
        in_specs=[hbm] * 3,
        out_specs=vmem,
        out_shape=jax.ShapeDtypeStruct((tok + ID_ROWS, 4 * DH), jnp.bfloat16),
        scratch_shapes=[pltpu.VMEM((1, tok), jnp.int32), pltpu.SemaphoreType.DMA((5,))],
        compiler_params=small,
        name="pack_halo",
    )(*(pltpu.with_memory_space_constraint(x, pltpu.HBM) for x in (ids, keys, values)))
    one, two = shifted(sent, 1), shifted(sent, 2)
    q, c, _ = lax.optimization_barrier((q, c, sent))
    rows = pl.pallas_call(
        pack_rows,
        in_specs=[hbm] * 2,
        out_specs=vmem,
        out_shape=jax.ShapeDtypeStruct((2 * tok, 2 * WIDE), jnp.bfloat16),
        scratch_shapes=[pltpu.SemaphoreType.DMA((4,))],
        compiler_params=small,
        name="pack_rows",
    )(*(pltpu.with_memory_space_constraint(x, pltpu.HBM) for x in (q, c)))
    rows = other_core(rows)
    place = jnp.stack([core, y_lo, (me % ROW < 1).astype(core.dtype), (me % ROW < 2).astype(core.dtype)])
    place = place.astype(jnp.int32)
    bias = pl.pallas_call(
        mask,
        in_specs=[vmem] * 3,
        out_specs=vmem,
        out_shape=jax.ShapeDtypeStruct((3 * tok, tok), jnp.float32),
        compiler_params=small,
        cost_estimate=pl.CostEstimate(flops=MASK_FLOPS, bytes_accessed=0, transcendentals=0),
        name="mask",
    )(ids, one, two)
    own_q, other_q, part = pl.pallas_call(
        attend,
        grid=(2,),
        in_specs=[pl.BlockSpec(memory_space=pltpu.SMEM)] + [vmem] * 8,
        out_specs=(vmem,) * 3,
        out_shape=(
            jax.ShapeDtypeStruct((tok, 2 * WIDE), jnp.bfloat16),
            jax.ShapeDtypeStruct((tok, 2 * WIDE), jnp.bfloat16),
            jax.ShapeDtypeStruct((4, 3 * tok, DH), jnp.bfloat16),
        ),
        compiler_params=pltpu.CompilerParams(vmem_limit_bytes=24 * 1024 * 1024),
        name="attend",
    )(place, bias, q, c, rows, keys, values, one, two)
    shares = [to_owner(part[step], step) for step in range(4)]
    total = sum(share[:tok].astype(jnp.float32) for share in shares)
    back = sum(share[tok:].astype(jnp.float32) for share in shares).astype(jnp.bfloat16)
    back = returned(back)
    swapped = other_core(jnp.concatenate([other_q, jnp.where(core == 0, back[tok:], back[:tok])], 1))
    grad_q, grad_k, grad_v = pl.pallas_call(
        finish,
        in_specs=[vmem] * 4,
        out_specs=(hbm, hbm, hbm),
        out_shape=(
            jax.ShapeDtypeStruct(q.shape, jnp.bfloat16),
            jax.ShapeDtypeStruct((DH // 2, tok), jnp.float32),
            jax.ShapeDtypeStruct((DH // 2, tok), jnp.float32),
        ),
        scratch_shapes=[pltpu.VMEM((DH, tok), jnp.float32), pltpu.SemaphoreType.DMA((6,))],
        compiler_params=small,
        name="finish",
    )(total, back, swapped, own_q)
    return (grad_q[None], grad_k.T, grad_v.T)


def solution(mesh):
    placed = (
        P("section", "ctx", None),
        P("ctx", None),
        P("ctx", None),
        P("section", "ctx", None),
        P("ctx"),
    )
    return jax.shard_map(
        on_device,
        mesh=mesh,
        in_specs=placed,
        out_specs=(P("section", "ctx", None), P("ctx", "section"), P("ctx", "section")),
        check_vma=False,
    )
```

```python
import jax
import jax.numpy as jnp
from jax import lax
from jax.experimental import pallas as pl
from jax.experimental.pallas import tpu as pltpu
from jax.sharding import PartitionSpec as P

DH = 128
TOK = 128
RATIO = 5
WIDE = RATIO * DH
ROW = 4
ID_ROWS = 16
SCALE = DH ** (-0.5)
LOG2E = 1.4426950408889634
NEG = -1e30
MASK_FLOPS = 9 << 29
AXES = ("section", "ctx")
NT = (((1,), (1,)), ((), ()))
TN = (((0,), (0,)), ((), ()))


def permuted(x, target):
    sections, cycle = lax.axis_size("section"), lax.axis_size("ctx")
    found = []
    for s in range(sections):
        for c in range(cycle):
            to = target(s, c)
            if 0 <= to[1] < cycle:
                found.append((s * cycle + c, to[0] * cycle + to[1]))
    return lax.ppermute(x, AXES, found)


def shifted(x, by, places=range(ROW)):
    def target(s, c):
        if (c + by) % ROW not in places:
            return (s, -1)
        leaves = c // ROW != (c + by) // ROW
        return ((3 - s // 2) * 2 + s % 2 if leaves else s, c + by)

    return permuted(x, target)


def returned(x):
    def target(s, c):
        to = c - 1 - s % 2
        return ((3 - s // 2) * 2 + s % 2 if c // ROW != to // ROW else s, to)

    return permuted(x, target)


def other_core(x):
    return permuted(x, lambda s, c: (s ^ 1, c))


def group_of(core, slot):
    return core + slot * (3 - 2 * core)


def to_owner(x, step):
    def target(s, c):
        share = (s // 2) ^ step
        return (group_of(s % 2, share // 2) * 2 + share % 2, c)

    return permuted(x, target)


def core_groups(core):
    return [group_of(core, slot) for slot in range(2)]


def columns(group, width):
    return pl.ds(pl.multiple_of(group * width, width), width)


def run(copies):
    for copy in copies:
        copy.start()
    for copy in copies:
        copy.wait()


def pack_halo(ids_ref, k_ref, v_ref, out_ref, ids_vmem, sems):
    copies = [pltpu.make_async_copy(ids_ref, ids_vmem, sems.at[4])]
    for slot, group in enumerate(core_groups(lax.axis_index("section") % 2)):
        for i, ref in enumerate((k_ref, v_ref)):
            to = out_ref.at[pl.ds((2 * slot + i) * TOK, TOK)]
            copies.append(pltpu.make_async_copy(ref.at[:, columns(group, DH)], to, sems.at[2 * slot + i]))
    run(copies)
    ids = jnp.broadcast_to((ids_vmem[...] + 1).astype(jnp.float32), (ID_ROWS, TOK))
    out_ref[4 * TOK :] = ids.astype(jnp.bfloat16)


def pack_rows(q_ref, c_ref, out_ref, sems):
    copies = []
    for slot, group in enumerate(core_groups(1 - lax.axis_index("section") % 2)):
        for i, ref in enumerate((q_ref, c_ref)):
            to = out_ref.at[pl.ds(i * TOK, TOK), pl.ds(slot * WIDE, WIDE)]
            copies.append(pltpu.make_async_copy(ref.at[:, columns(group, WIDE)], to, sems.at[2 * slot + i]))
    run(copies)


def mask(ids_ref, one_ref, two_ref, relay_ref, out_ref):
    ids = ids_ref[...].astype(jnp.float32)
    first = ids[:, 0:1]
    row = lax.broadcasted_iota(jnp.int32, (TOK, TOK), 0)
    col = lax.broadcasted_iota(jnp.int32, (TOK, TOK), 1)
    wide = jnp.broadcast_to(ids, (TOK, TOK))
    out_ref[:TOK] = jnp.where((wide.T == wide) & (row <= col), 0.0, NEG)
    for block, halos in enumerate(((one_ref,), (two_ref, relay_ref))):
        before = sum(halo[4 * TOK :].astype(jnp.float32)[0:1] for halo in halos)
        held = jnp.sum(jnp.where(before == first + 1.0, 1.0, 0.0), -1, keepdims=True)
        out_ref[(block + 1) * TOK : (block + 2) * TOK] = jnp.where(
            (wide == first) & (row.astype(jnp.float32) >= TOK - held), 0.0, NEG
        )


def attend(
    place_ref, bias_ref, q_ref, c_ref, oqc_ref, k_ref, v_ref, one_ref, two_ref, relay_ref, dq_ref, odq_ref, part_ref
):
    slot = pl.program_id(0)
    group = group_of(place_ref[0], slot)

    def lanes(start, size=DH):
        return pl.ds(pl.multiple_of(start, DH), size)

    def rows(i):
        return pl.ds(pl.multiple_of((2 * slot + i) * TOK, TOK), TOK)

    keys, values = [
        jnp.concatenate([ref[:, lanes(group * DH)], one_ref[rows(i)], two_ref[rows(i)] + relay_ref[rows(i)]], 0)
        for i, ref in enumerate((k_ref, v_ref))
    ]
    bias = bias_ref[...]
    grad_k = jnp.zeros((3 * TOK, DH), jnp.float32)
    grad_v = jnp.zeros((3 * TOK, DH), jnp.float32)
    for mine in (True, False):
        start = (group if mine else slot) * WIDE
        queries, cots = [], []
        for h in range(RATIO):
            at = lanes(start + h * DH)
            queries.append(q_ref[:, at] if mine else oqc_ref[:TOK, at])
            cots.append(c_ref[:, at] if mine else oqc_ref[TOK:, at])
        queries, cots = jnp.concatenate(queries, 0), jnp.concatenate(cots, 0)
        scores = lax.dot_general(keys, queries, NT, preferred_element_type=jnp.float32)
        grad_probs = lax.dot_general(values, cots, NT, preferred_element_type=jnp.float32)
        probs_low, scaled_low = [], []
        for h in range(RATIO):
            at = slice(h * TOK, (h + 1) * TOK)
            s = scores[:, at] * (SCALE * LOG2E) + bias
            e = jnp.exp2(s - jnp.max(s, 0, keepdims=True))
            p = e * (1.0 / jnp.sum(e, 0, keepdims=True))
            low = p.astype(jnp.bfloat16)
            g = grad_probs[:, at]
            dot = jnp.sum(low.astype(jnp.float32) * g, 0, keepdims=True)
            probs_low.append(low)
            scaled_low.append((p * (g - dot) * SCALE).astype(jnp.bfloat16))
        probs_low = jnp.concatenate(probs_low, 1)
        scaled_low = jnp.concatenate(scaled_low, 1)
        grad_v += jnp.dot(probs_low, cots, preferred_element_type=jnp.float32)
        grad_k += jnp.dot(scaled_low, queries, preferred_element_type=jnp.float32)
        grad_q = lax.dot_general(keys, scaled_low, TN, preferred_element_type=jnp.float32)
        out = dq_ref if mine else odq_ref
        for h in range(RATIO):
            out[:, lanes(slot * WIDE + h * DH)] = grad_q[:, h * TOK : (h + 1) * TOK].T.astype(jnp.bfloat16)
    half = DH // 2
    grad_k = grad_k.astype(jnp.bfloat16)
    grad_v = grad_v.astype(jnp.bfloat16)
    shares = (
        jnp.concatenate([grad_k[:, :half], grad_v[:, :half]], 1),
        jnp.concatenate([grad_k[:, half:], grad_v[:, half:]], 1),
    )
    for side in range(2):
        part_ref[(2 * slot + side) ^ place_ref[1], :TOK, :] = shares[side][:TOK]
        for block in (1, 2):
            carrier = 2 * (slot ^ place_ref[1 + block]) + block - 1
            at = slice((1 + side) * TOK, (2 + side) * TOK)
            part_ref[carrier ^ place_ref[1], at, :] = shares[side][block * TOK : (block + 1) * TOK]


def finish(own_ref, back_ref, swapped_ref, own_q_ref, dq_ref, dk_ref, dv_ref, total_ref, sems):
    core = lax.axis_index("section") % 2
    half = DH // 2
    copies = []
    for i, ref in enumerate((own_q_ref, swapped_ref)):
        for slot, group in enumerate(core_groups(core if i == 0 else 1 - core)):
            src = ref.at[:, pl.ds(slot * WIDE, WIDE)]
            copies.append(pltpu.make_async_copy(src, dq_ref.at[:, columns(group, WIDE)], sems.at[2 * i + slot]))
    for copy in copies:
        copy.start()
    mine = back_ref[pl.ds(pl.multiple_of(core * TOK, TOK), TOK), :]
    total = own_ref[...] + mine.astype(jnp.float32) + swapped_ref[:, 2 * WIDE :].astype(jnp.float32)
    total_ref[...] = total.T
    for i, ref in enumerate((dk_ref, dv_ref)):
        copies.append(pltpu.make_async_copy(total_ref.at[pl.ds(i * half, half)], ref, sems.at[4 + i]))
        copies[-1].start()
    for copy in copies:
        copy.wait()


def on_device(queries, keys, values, cotangent, segment_ids):
    section, me = lax.axis_index("section"), lax.axis_index("ctx")
    core, y_lo = section % 2, section // 2
    tok = keys.shape[0]
    q, c = queries[0], cotangent[0]
    ids = segment_ids.reshape(1, tok)
    hbm = pl.BlockSpec(memory_space=pltpu.HBM)
    vmem = pl.BlockSpec(memory_space=pltpu.VMEM)

    small = pltpu.CompilerParams(vmem_limit_bytes=4 * 1024 * 1024)

    sent = pl.pallas_call(
        pack_halo,
        in_specs=[hbm] * 3,
        out_specs=vmem,
        out_shape=jax.ShapeDtypeStruct((4 * tok + ID_ROWS, DH), jnp.bfloat16),
        scratch_shapes=[pltpu.VMEM((1, tok), jnp.int32), pltpu.SemaphoreType.DMA((5,))],
        compiler_params=small,
        name="pack_halo",
    )(*(pltpu.with_memory_space_constraint(x, pltpu.HBM) for x in (ids, keys, values)))
    one, two = shifted(sent, 1), shifted(sent, 2, (0, 2, 3))
    relay = shifted(one, 1, (1,))
    q, c, _ = lax.optimization_barrier((q, c, sent))
    rows = pl.pallas_call(
        pack_rows,
        in_specs=[hbm] * 2,
        out_specs=vmem,
        out_shape=jax.ShapeDtypeStruct((2 * tok, 2 * WIDE), jnp.bfloat16),
        scratch_shapes=[pltpu.SemaphoreType.DMA((4,))],
        compiler_params=small,
        name="pack_rows",
    )(*(pltpu.with_memory_space_constraint(x, pltpu.HBM) for x in (q, c)))
    rows = other_core(rows)
    place = jnp.stack([core, y_lo, (me % ROW < 1).astype(core.dtype), (me % ROW < 2).astype(core.dtype)])
    place = place.astype(jnp.int32)
    bias = pl.pallas_call(
        mask,
        in_specs=[vmem] * 4,
        out_specs=vmem,
        out_shape=jax.ShapeDtypeStruct((3 * tok, tok), jnp.float32),
        compiler_params=small,
        cost_estimate=pl.CostEstimate(flops=MASK_FLOPS, bytes_accessed=0, transcendentals=0),
        name="mask",
    )(ids, one, two, relay)
    own_q, other_q, part = pl.pallas_call(
        attend,
        grid=(2,),
        in_specs=[pl.BlockSpec(memory_space=pltpu.SMEM)] + [vmem] * 9,
        out_specs=(vmem,) * 3,
        out_shape=(
            jax.ShapeDtypeStruct((tok, 2 * WIDE), jnp.bfloat16),
            jax.ShapeDtypeStruct((tok, 2 * WIDE), jnp.bfloat16),
            jax.ShapeDtypeStruct((4, 3 * tok, DH), jnp.bfloat16),
        ),
        compiler_params=pltpu.CompilerParams(vmem_limit_bytes=24 * 1024 * 1024),
        name="attend",
    )(place, bias, q, c, rows, keys, values, one, two, relay)
    shares = [to_owner(part[step], step) for step in range(4)]
    total = sum(share[:tok].astype(jnp.float32) for share in shares)
    back = sum(share[tok:].astype(jnp.float32) for share in shares).astype(jnp.bfloat16)
    back = returned(back)
    swapped = other_core(jnp.concatenate([other_q, jnp.where(core == 0, back[tok:], back[:tok])], 1))
    grad_q, grad_k, grad_v = pl.pallas_call(
        finish,
        in_specs=[vmem] * 4,
        out_specs=(hbm, hbm, hbm),
        out_shape=(
            jax.ShapeDtypeStruct(q.shape, jnp.bfloat16),
            jax.ShapeDtypeStruct((DH // 2, tok), jnp.float32),
            jax.ShapeDtypeStruct((DH // 2, tok), jnp.float32),
        ),
        scratch_shapes=[pltpu.VMEM((DH, tok), jnp.float32), pltpu.SemaphoreType.DMA((6,))],
        compiler_params=small,
        name="finish",
    )(total, back, swapped, own_q)
    return (grad_q[None], grad_k.T, grad_v.T)


def solution(mesh):
    placed = (
        P("section", "ctx", None),
        P("ctx", None),
        P("ctx", None),
        P("section", "ctx", None),
        P("ctx"),
    )
    return jax.shard_map(
        on_device,
        mesh=mesh,
        in_specs=placed,
        out_specs=(P("section", "ctx", None), P("ctx", "section"), P("ctx", "section")),
        check_vma=False,
    )
```

```python
import jax
import jax.numpy as jnp
from jax import lax
from jax.experimental import pallas as pl
from jax.experimental.pallas import tpu as pltpu
from jax.sharding import PartitionSpec as P

DH = 128
TOK = 128
RATIO = 5
WIDE = RATIO * DH
ROW = 4
ID_ROWS = 16
SCALE = DH ** (-0.5)
LOG2E = 1.4426950408889634
NEG = -1e30
MASK_FLOPS = 1 << 34
AXES = ("section", "ctx")
NT = (((1,), (1,)), ((), ()))
TN = (((0,), (0,)), ((), ()))


def permuted(x, target):
    sections, cycle = lax.axis_size("section"), lax.axis_size("ctx")
    found = []
    for s in range(sections):
        for c in range(cycle):
            to = target(s, c)
            if 0 <= to[1] < cycle:
                found.append((s * cycle + c, to[0] * cycle + to[1]))
    return lax.ppermute(x, AXES, found)


def shifted(x, by, places=range(ROW)):
    def target(s, c):
        if (c + by) % ROW not in places:
            return (s, -1)
        leaves = c // ROW != (c + by) // ROW
        return ((3 - s // 2) * 2 + s % 2 if leaves else s, c + by)

    return permuted(x, target)


def returned(x):
    def target(s, c):
        to = c - 1 - s % 2
        return ((3 - s // 2) * 2 + s % 2 if c // ROW != to // ROW else s, to)

    return permuted(x, target)


def other_core(x):
    return permuted(x, lambda s, c: (s ^ 1, c))


def group_of(core, slot):
    return core + slot * (3 - 2 * core)


def to_owner(x, step):
    def target(s, c):
        share = (s // 2) ^ step
        return (group_of(s % 2, share // 2) * 2 + share % 2, c)

    return permuted(x, target)


def core_groups(core):
    return [group_of(core, slot) for slot in range(2)]


def columns(group, width):
    return pl.ds(pl.multiple_of(group * width, width), width)


def run(copies):
    for copy in copies:
        copy.start()
    for copy in copies:
        copy.wait()


def pack_halo(ids_ref, k_ref, v_ref, out_ref, ids_vmem, sems):
    copies = [pltpu.make_async_copy(ids_ref, ids_vmem, sems.at[4])]
    for slot, group in enumerate(core_groups(lax.axis_index("section") % 2)):
        for i, ref in enumerate((k_ref, v_ref)):
            to = out_ref.at[pl.ds((2 * slot + i) * TOK, TOK)]
            copies.append(pltpu.make_async_copy(ref.at[:, columns(group, DH)], to, sems.at[2 * slot + i]))
    run(copies)
    ids = jnp.broadcast_to((ids_vmem[...] + 1).astype(jnp.float32), (ID_ROWS, TOK))
    out_ref[4 * TOK :] = ids.astype(jnp.bfloat16)


def pack_rows(q_ref, c_ref, out_ref, sems):
    copies = []
    for slot, group in enumerate(core_groups(1 - lax.axis_index("section") % 2)):
        for i, ref in enumerate((q_ref, c_ref)):
            to = out_ref.at[pl.ds(i * TOK, TOK), pl.ds(slot * WIDE, WIDE)]
            copies.append(pltpu.make_async_copy(ref.at[:, columns(group, WIDE)], to, sems.at[2 * slot + i]))
    run(copies)


def halo_mask(ids, *halos):
    first = ids[:, 0:1]
    before = sum(halo[4 * TOK :].astype(jnp.float32)[0:1] for halo in halos)
    held = jnp.sum(jnp.where(before == first + 1.0, 1.0, 0.0), -1, keepdims=True)
    row = lax.broadcasted_iota(jnp.int32, (TOK, TOK), 0).astype(jnp.float32)
    wide = jnp.broadcast_to(ids, (TOK, TOK))
    return jnp.where((wide == first) & (row >= TOK - held), 0.0, NEG)


def mask_near(ids_ref, one_ref, out_ref):
    ids = ids_ref[...].astype(jnp.float32)
    row = lax.broadcasted_iota(jnp.int32, (TOK, TOK), 0)
    col = lax.broadcasted_iota(jnp.int32, (TOK, TOK), 1)
    wide = jnp.broadcast_to(ids, (TOK, TOK))
    out_ref[:TOK] = jnp.where((wide.T == wide) & (row <= col), 0.0, NEG)
    out_ref[TOK:] = halo_mask(ids, one_ref)


def mask_far(ids_ref, two_ref, relay_ref, out_ref):
    out_ref[...] = halo_mask(ids_ref[...].astype(jnp.float32), two_ref, relay_ref)


def attend(
    place_ref, near_ref, far_ref, q_ref, c_ref, oqc_ref, k_ref, v_ref, one_ref, two_ref, relay_ref, dq_ref, odq_ref, part_ref
):
    slot = pl.program_id(0)
    group = group_of(place_ref[0], slot)

    def lanes(start, size=DH):
        return pl.ds(pl.multiple_of(start, DH), size)

    def rows(i):
        return pl.ds(pl.multiple_of((2 * slot + i) * TOK, TOK), TOK)

    keys, values = [
        jnp.concatenate([ref[:, lanes(group * DH)], one_ref[rows(i)], two_ref[rows(i)] + relay_ref[rows(i)]], 0)
        for i, ref in enumerate((k_ref, v_ref))
    ]
    bias = jnp.concatenate([near_ref[...], far_ref[...]], 0)
    grad_k = jnp.zeros((3 * TOK, DH), jnp.float32)
    grad_v = jnp.zeros((3 * TOK, DH), jnp.float32)
    for mine in (True, False):
        start = (group if mine else slot) * WIDE
        queries, cots = [], []
        for h in range(RATIO):
            at = lanes(start + h * DH)
            queries.append(q_ref[:, at] if mine else oqc_ref[:TOK, at])
            cots.append(c_ref[:, at] if mine else oqc_ref[TOK:, at])
        queries, cots = jnp.concatenate(queries, 0), jnp.concatenate(cots, 0)
        scores = lax.dot_general(keys, queries, NT, preferred_element_type=jnp.float32)
        grad_probs = lax.dot_general(values, cots, NT, preferred_element_type=jnp.float32)
        probs_low, scaled_low = [], []
        for h in range(RATIO):
            at = slice(h * TOK, (h + 1) * TOK)
            s = scores[:, at] * (SCALE * LOG2E) + bias
            e = jnp.exp2(s - jnp.max(s, 0, keepdims=True))
            p = e * (1.0 / jnp.sum(e, 0, keepdims=True))
            low = p.astype(jnp.bfloat16)
            g = grad_probs[:, at]
            dot = jnp.sum(low.astype(jnp.float32) * g, 0, keepdims=True)
            probs_low.append(low)
            scaled_low.append((p * (g - dot) * SCALE).astype(jnp.bfloat16))
        probs_low = jnp.concatenate(probs_low, 1)
        scaled_low = jnp.concatenate(scaled_low, 1)
        grad_v += jnp.dot(probs_low, cots, preferred_element_type=jnp.float32)
        grad_k += jnp.dot(scaled_low, queries, preferred_element_type=jnp.float32)
        grad_q = lax.dot_general(keys, scaled_low, TN, preferred_element_type=jnp.float32)
        out = dq_ref if mine else odq_ref
        for h in range(RATIO):
            out[:, lanes(slot * WIDE + h * DH)] = grad_q[:, h * TOK : (h + 1) * TOK].T.astype(jnp.bfloat16)
    half = DH // 2
    grad_k = grad_k.astype(jnp.bfloat16)
    grad_v = grad_v.astype(jnp.bfloat16)
    shares = (
        jnp.concatenate([grad_k[:, :half], grad_v[:, :half]], 1),
        jnp.concatenate([grad_k[:, half:], grad_v[:, half:]], 1),
    )
    for side in range(2):
        part_ref[(2 * slot + side) ^ place_ref[1], :TOK, :] = shares[side][:TOK]
        for block in (1, 2):
            carrier = 2 * (slot ^ place_ref[1 + block]) + block - 1
            at = slice((1 + side) * TOK, (2 + side) * TOK)
            part_ref[carrier ^ place_ref[1], at, :] = shares[side][block * TOK : (block + 1) * TOK]


def finish(own_ref, back_ref, swapped_ref, own_q_ref, dq_ref, dk_ref, dv_ref, total_ref, sems):
    core = lax.axis_index("section") % 2
    half = DH // 2
    copies = []
    for i, ref in enumerate((own_q_ref, swapped_ref)):
        for slot, group in enumerate(core_groups(core if i == 0 else 1 - core)):
            src = ref.at[:, pl.ds(slot * WIDE, WIDE)]
            copies.append(pltpu.make_async_copy(src, dq_ref.at[:, columns(group, WIDE)], sems.at[2 * i + slot]))
    for copy in copies:
        copy.start()
    mine = back_ref[pl.ds(pl.multiple_of(core * TOK, TOK), TOK), :]
    total = own_ref[...] + mine.astype(jnp.float32) + swapped_ref[:, 2 * WIDE :].astype(jnp.float32)
    total_ref[...] = total.T
    for i, ref in enumerate((dk_ref, dv_ref)):
        copies.append(pltpu.make_async_copy(total_ref.at[pl.ds(i * half, half)], ref, sems.at[4 + i]))
        copies[-1].start()
    for copy in copies:
        copy.wait()


def on_device(queries, keys, values, cotangent, segment_ids):
    section, me = lax.axis_index("section"), lax.axis_index("ctx")
    core, y_lo = section % 2, section // 2
    tok = keys.shape[0]
    q, c = queries[0], cotangent[0]
    ids = segment_ids.reshape(1, tok)
    hbm = pl.BlockSpec(memory_space=pltpu.HBM)
    vmem = pl.BlockSpec(memory_space=pltpu.VMEM)

    small = pltpu.CompilerParams(vmem_limit_bytes=4 * 1024 * 1024)

    sent = pl.pallas_call(
        pack_halo,
        in_specs=[hbm] * 3,
        out_specs=vmem,
        out_shape=jax.ShapeDtypeStruct((4 * tok + ID_ROWS, DH), jnp.bfloat16),
        scratch_shapes=[pltpu.VMEM((1, tok), jnp.int32), pltpu.SemaphoreType.DMA((5,))],
        compiler_params=small,
        name="pack_halo",
    )(*(pltpu.with_memory_space_constraint(x, pltpu.HBM) for x in (ids, keys, values)))
    one, two = shifted(sent, 1), shifted(sent, 2, (0, 2, 3))
    q, c, _ = lax.optimization_barrier((q, c, sent))
    rows = pl.pallas_call(
        pack_rows,
        in_specs=[hbm] * 2,
        out_specs=vmem,
        out_shape=jax.ShapeDtypeStruct((2 * tok, 2 * WIDE), jnp.bfloat16),
        scratch_shapes=[pltpu.SemaphoreType.DMA((4,))],
        compiler_params=small,
        name="pack_rows",
    )(*(pltpu.with_memory_space_constraint(x, pltpu.HBM) for x in (q, c)))
    rows = other_core(rows)
    near = pl.pallas_call(
        mask_near,
        in_specs=[vmem] * 2,
        out_specs=vmem,
        out_shape=jax.ShapeDtypeStruct((2 * tok, tok), jnp.float32),
        compiler_params=small,
        cost_estimate=pl.CostEstimate(flops=MASK_FLOPS, bytes_accessed=0, transcendentals=0),
        name="mask_near",
    )(ids, one)
    one, rows, near = lax.optimization_barrier((one, rows, near))
    relay = shifted(one, 1, (1,))
    place = jnp.stack([core, y_lo, (me % ROW < 1).astype(core.dtype), (me % ROW < 2).astype(core.dtype)])
    place = place.astype(jnp.int32)
    far = pl.pallas_call(
        mask_far,
        in_specs=[vmem] * 3,
        out_specs=vmem,
        out_shape=jax.ShapeDtypeStruct((tok, tok), jnp.float32),
        compiler_params=small,
        name="mask_far",
    )(ids, two, relay)
    own_q, other_q, part = pl.pallas_call(
        attend,
        grid=(2,),
        in_specs=[pl.BlockSpec(memory_space=pltpu.SMEM)] + [vmem] * 10,
        out_specs=(vmem,) * 3,
        out_shape=(
            jax.ShapeDtypeStruct((tok, 2 * WIDE), jnp.bfloat16),
            jax.ShapeDtypeStruct((tok, 2 * WIDE), jnp.bfloat16),
            jax.ShapeDtypeStruct((4, 3 * tok, DH), jnp.bfloat16),
        ),
        compiler_params=pltpu.CompilerParams(vmem_limit_bytes=24 * 1024 * 1024),
        name="attend",
    )(place, near, far, q, c, rows, keys, values, one, two, relay)
    shares = [to_owner(part[step], step) for step in range(4)]
    total = sum(share[:tok].astype(jnp.float32) for share in shares)
    back = sum(share[tok:].astype(jnp.float32) for share in shares).astype(jnp.bfloat16)
    back = returned(back)
    swapped = other_core(jnp.concatenate([other_q, jnp.where(core == 0, back[tok:], back[:tok])], 1))
    grad_q, grad_k, grad_v = pl.pallas_call(
        finish,
        in_specs=[vmem] * 4,
        out_specs=(hbm, hbm, hbm),
        out_shape=(
            jax.ShapeDtypeStruct(q.shape, jnp.bfloat16),
            jax.ShapeDtypeStruct((DH // 2, tok), jnp.float32),
            jax.ShapeDtypeStruct((DH // 2, tok), jnp.float32),
        ),
        scratch_shapes=[pltpu.VMEM((DH, tok), jnp.float32), pltpu.SemaphoreType.DMA((6,))],
        compiler_params=small,
        name="finish",
    )(total, back, swapped, own_q)
    return (grad_q[None], grad_k.T, grad_v.T)


def solution(mesh):
    placed = (
        P("section", "ctx", None),
        P("ctx", None),
        P("ctx", None),
        P("section", "ctx", None),
        P("ctx"),
    )
    return jax.shard_map(
        on_device,
        mesh=mesh,
        in_specs=placed,
        out_specs=(P("section", "ctx", None), P("ctx", "section"), P("ctx", "section")),
        check_vma=False,
    )
```

```python
import jax
import jax.numpy as jnp
from jax import lax
from jax.experimental import pallas as pl
from jax.experimental.pallas import tpu as pltpu
from jax.sharding import PartitionSpec as P

DH = 128
TOK = 128
RATIO = 5
WIDE = RATIO * DH
ROW = 4
ID_ROWS = 16
SCALE = DH ** (-0.5)
LOG2E = 1.4426950408889634
NEG = -1e30
FAR_FLOPS = 1 << 31
NEAR_FLOPS = 1 << 33
AXES = ("section", "ctx")
NT = (((1,), (1,)), ((), ()))
TN = (((0,), (0,)), ((), ()))


def permuted(x, target):
    sections, cycle = lax.axis_size("section"), lax.axis_size("ctx")
    found = []
    for s in range(sections):
        for c in range(cycle):
            to = target(s, c)
            if 0 <= to[1] < cycle:
                found.append((s * cycle + c, to[0] * cycle + to[1]))
    return lax.ppermute(x, AXES, found)


def shifted(x, by, places=range(ROW)):
    def target(s, c):
        if (c + by) % ROW not in places:
            return (s, -1)
        leaves = c // ROW != (c + by) // ROW
        return ((3 - s // 2) * 2 + s % 2 if leaves else s, c + by)

    return permuted(x, target)


def returned(x):
    def target(s, c):
        share = s // 2
        chip, to = group_of(s % 2, share // 2), c - 1 - share % 2
        return ((3 - chip if c // ROW != to // ROW else chip) * 2 + share % 2, to)

    return permuted(x, target)


def other_core(x):
    return permuted(x, lambda s, c: (s ^ 1, c))


def group_of(core, slot):
    return core + slot * (3 - 2 * core)


def to_owner(x):
    return permuted(x, lambda s, c: (group_of(s % 2, s // 2 // 2) * 2 + s // 2 % 2, c))


def core_groups(core):
    return [group_of(core, slot) for slot in range(2)]


def columns(group, width):
    return pl.ds(pl.multiple_of(group * width, width), width)


def run(copies):
    for copy in copies:
        copy.start()
    for copy in copies:
        copy.wait()


def pack_halo(ids_ref, k_ref, v_ref, out_ref, ids_vmem, sems):
    copies = [pltpu.make_async_copy(ids_ref, ids_vmem, sems.at[4])]
    for slot, group in enumerate(core_groups(lax.axis_index("section") % 2)):
        for i, ref in enumerate((k_ref, v_ref)):
            to = out_ref.at[pl.ds((2 * slot + i) * TOK, TOK)]
            copies.append(pltpu.make_async_copy(ref.at[:, columns(group, DH)], to, sems.at[2 * slot + i]))
    run(copies)
    ids = jnp.broadcast_to((ids_vmem[...] + 1).astype(jnp.float32), (ID_ROWS, TOK))
    out_ref[4 * TOK :] = ids.astype(jnp.bfloat16)


def pack_rows(q_ref, c_ref, out_ref, sems):
    copies = []
    for slot, group in enumerate(core_groups(1 - lax.axis_index("section") % 2)):
        for i, ref in enumerate((q_ref, c_ref)):
            to = out_ref.at[pl.ds(i * TOK, TOK), pl.ds(slot * WIDE, WIDE)]
            copies.append(pltpu.make_async_copy(ref.at[:, columns(group, WIDE)], to, sems.at[2 * slot + i]))
    run(copies)


def halo_mask(ids, *halos):
    first = ids[:, 0:1]
    before = sum(halo[4 * TOK :].astype(jnp.float32)[0:1] for halo in halos)
    held = jnp.sum(jnp.where(before == first + 1.0, 1.0, 0.0), -1, keepdims=True)
    row = lax.broadcasted_iota(jnp.int32, (TOK, TOK), 0).astype(jnp.float32)
    wide = jnp.broadcast_to(ids, (TOK, TOK))
    return jnp.where((wide == first) & (row >= TOK - held), 0.0, NEG)


def mask_near(ids_ref, one_ref, out_ref):
    ids = ids_ref[...].astype(jnp.float32)
    row = lax.broadcasted_iota(jnp.int32, (TOK, TOK), 0)
    col = lax.broadcasted_iota(jnp.int32, (TOK, TOK), 1)
    wide = jnp.broadcast_to(ids, (TOK, TOK))
    out_ref[:TOK] = jnp.where((wide.T == wide) & (row <= col), 0.0, NEG)
    out_ref[TOK:] = halo_mask(ids, one_ref)


def mask_far(ids_ref, two_ref, relay_ref, out_ref):
    out_ref[...] = halo_mask(ids_ref[...].astype(jnp.float32), two_ref, relay_ref)


def attend(
    place_ref, near_ref, far_ref, q_ref, c_ref, oqc_ref, k_ref, v_ref, one_ref, two_ref, relay_ref, dq_ref, odq_ref, part_ref
):
    slot = pl.program_id(0)
    group = group_of(place_ref[0], slot)

    def lanes(start, size=DH):
        return pl.ds(pl.multiple_of(start, DH), size)

    def rows(i):
        return pl.ds(pl.multiple_of((2 * slot + i) * TOK, TOK), TOK)

    keys, values = [
        jnp.concatenate([ref[:, lanes(group * DH)], one_ref[rows(i)], two_ref[rows(i)] + relay_ref[rows(i)]], 0)
        for i, ref in enumerate((k_ref, v_ref))
    ]
    bias = jnp.concatenate([near_ref[...], far_ref[...]], 0)
    grad_k = jnp.zeros((3 * TOK, DH), jnp.float32)
    grad_v = jnp.zeros((3 * TOK, DH), jnp.float32)
    for mine in (True, False):
        start = (group if mine else slot) * WIDE
        queries, cots = [], []
        for h in range(RATIO):
            at = lanes(start + h * DH)
            queries.append(q_ref[:, at] if mine else oqc_ref[:TOK, at])
            cots.append(c_ref[:, at] if mine else oqc_ref[TOK:, at])
        queries, cots = jnp.concatenate(queries, 0), jnp.concatenate(cots, 0)
        scores = lax.dot_general(keys, queries, NT, preferred_element_type=jnp.float32)
        grad_probs = lax.dot_general(values, cots, NT, preferred_element_type=jnp.float32)
        probs_low, scaled_low = [], []
        for h in range(RATIO):
            at = slice(h * TOK, (h + 1) * TOK)
            s = scores[:, at] * (SCALE * LOG2E) + bias
            e = jnp.exp2(s - jnp.max(s, 0, keepdims=True))
            p = e * (1.0 / jnp.sum(e, 0, keepdims=True))
            low = p.astype(jnp.bfloat16)
            g = grad_probs[:, at]
            dot = jnp.sum(low.astype(jnp.float32) * g, 0, keepdims=True)
            probs_low.append(low)
            scaled_low.append((p * (g - dot) * SCALE).astype(jnp.bfloat16))
        probs_low = jnp.concatenate(probs_low, 1)
        scaled_low = jnp.concatenate(scaled_low, 1)
        grad_v += jnp.dot(probs_low, cots, preferred_element_type=jnp.float32)
        grad_k += jnp.dot(scaled_low, queries, preferred_element_type=jnp.float32)
        grad_q = lax.dot_general(keys, scaled_low, TN, preferred_element_type=jnp.float32)
        out = dq_ref if mine else odq_ref
        for h in range(RATIO):
            out[:, lanes(slot * WIDE + h * DH)] = grad_q[:, h * TOK : (h + 1) * TOK].T.astype(jnp.bfloat16)
    half = DH // 2
    grad_k = grad_k.astype(jnp.bfloat16)
    grad_v = grad_v.astype(jnp.bfloat16)
    shares = (
        jnp.concatenate([grad_k[:, :half], grad_v[:, :half]], 1),
        jnp.concatenate([grad_k[:, half:], grad_v[:, half:]], 1),
    )
    for side in range(2):
        part_ref[2 * slot + side, :TOK, :] = shares[side][:TOK]
        for block in (1, 2):
            carrier = 2 * (slot ^ place_ref[1 + block]) + block - 1
            at = slice((1 + side) * TOK, (2 + side) * TOK)
            part_ref[carrier, at, :] = shares[side][block * TOK : (block + 1) * TOK]


def finish(own_ref, back_ref, swapped_ref, own_q_ref, dq_ref, dk_ref, dv_ref, total_ref, sems):
    core = lax.axis_index("section") % 2
    half = DH // 2
    copies = []
    for i, ref in enumerate((own_q_ref, swapped_ref)):
        for slot, group in enumerate(core_groups(core if i == 0 else 1 - core)):
            src = ref.at[:, pl.ds(slot * WIDE, WIDE)]
            copies.append(pltpu.make_async_copy(src, dq_ref.at[:, columns(group, WIDE)], sems.at[2 * i + slot]))
    for copy in copies:
        copy.start()
    mine = back_ref[pl.ds(pl.multiple_of(core * TOK, TOK), TOK), :]
    total = own_ref[...].astype(jnp.float32) + mine.astype(jnp.float32) + swapped_ref[:, 2 * WIDE :].astype(jnp.float32)
    total_ref[...] = total.T
    for i, ref in enumerate((dk_ref, dv_ref)):
        copies.append(pltpu.make_async_copy(total_ref.at[pl.ds(i * half, half)], ref, sems.at[4 + i]))
        copies[-1].start()
    for copy in copies:
        copy.wait()


def on_device(queries, keys, values, cotangent, segment_ids):
    section, me = lax.axis_index("section"), lax.axis_index("ctx")
    core, y_lo = section % 2, section // 2
    tok = keys.shape[0]
    q, c = queries[0], cotangent[0]
    ids = segment_ids.reshape(1, tok)
    hbm = pl.BlockSpec(memory_space=pltpu.HBM)
    vmem = pl.BlockSpec(memory_space=pltpu.VMEM)

    small = pltpu.CompilerParams(vmem_limit_bytes=4 * 1024 * 1024)

    sent = pl.pallas_call(
        pack_halo,
        in_specs=[hbm] * 3,
        out_specs=vmem,
        out_shape=jax.ShapeDtypeStruct((4 * tok + ID_ROWS, DH), jnp.bfloat16),
        scratch_shapes=[pltpu.VMEM((1, tok), jnp.int32), pltpu.SemaphoreType.DMA((5,))],
        compiler_params=small,
        name="pack_halo",
    )(*(pltpu.with_memory_space_constraint(x, pltpu.HBM) for x in (ids, keys, values)))
    one, two = shifted(sent, 1), shifted(sent, 2, (0, 2, 3))
    q, c, _ = lax.optimization_barrier((q, c, sent))
    rows = pl.pallas_call(
        pack_rows,
        in_specs=[hbm] * 2,
        out_specs=vmem,
        out_shape=jax.ShapeDtypeStruct((2 * tok, 2 * WIDE), jnp.bfloat16),
        scratch_shapes=[pltpu.SemaphoreType.DMA((4,))],
        compiler_params=small,
        name="pack_rows",
    )(*(pltpu.with_memory_space_constraint(x, pltpu.HBM) for x in (q, c)))
    near = pl.pallas_call(
        mask_near,
        in_specs=[vmem] * 2,
        out_specs=vmem,
        out_shape=jax.ShapeDtypeStruct((2 * tok, tok), jnp.float32),
        compiler_params=small,
        cost_estimate=pl.CostEstimate(flops=NEAR_FLOPS, bytes_accessed=0, transcendentals=0),
        name="mask_near",
    )(ids, one)
    one, near = lax.optimization_barrier((one, near))
    relay = shifted(one, 1, (1,))
    rows = other_core(rows)
    place = jnp.stack([core, core, (me % ROW < 1).astype(core.dtype), (me % ROW < 2).astype(core.dtype)])
    place = place.astype(jnp.int32)
    far = pl.pallas_call(
        mask_far,
        in_specs=[vmem] * 3,
        out_specs=vmem,
        out_shape=jax.ShapeDtypeStruct((tok, tok), jnp.float32),
        compiler_params=small,
        cost_estimate=pl.CostEstimate(flops=FAR_FLOPS, bytes_accessed=0, transcendentals=0),
        name="mask_far",
    )(ids, two, relay)
    own_q, other_q, part = pl.pallas_call(
        attend,
        grid=(2,),
        in_specs=[pl.BlockSpec(memory_space=pltpu.SMEM)] + [vmem] * 10,
        out_specs=(vmem,) * 3,
        out_shape=(
            jax.ShapeDtypeStruct((tok, 2 * WIDE), jnp.bfloat16),
            jax.ShapeDtypeStruct((tok, 2 * WIDE), jnp.bfloat16),
            jax.ShapeDtypeStruct((4, 3 * tok, DH), jnp.bfloat16),
        ),
        compiler_params=pltpu.CompilerParams(vmem_limit_bytes=24 * 1024 * 1024),
        name="attend",
    )(place, near, far, q, c, rows, keys, values, one, two, relay)
    chips = [[s for s in range(8) if s % 2 == parity] for parity in range(2)]
    shares = lax.all_to_all(part, "section", 0, 0, axis_index_groups=chips)
    back = returned(jnp.sum(shares[:, tok:].astype(jnp.float32), 0).astype(jnp.bfloat16))
    total = to_owner(jnp.sum(shares[:, :tok].astype(jnp.float32), 0).astype(jnp.bfloat16))
    back, total = lax.optimization_barrier((back, total))
    swapped = other_core(jnp.concatenate([other_q, jnp.where(core == 0, back[tok:], back[:tok])], 1))
    grad_q, grad_k, grad_v = pl.pallas_call(
        finish,
        in_specs=[vmem] * 4,
        out_specs=(hbm, hbm, hbm),
        out_shape=(
            jax.ShapeDtypeStruct(q.shape, jnp.bfloat16),
            jax.ShapeDtypeStruct((DH // 2, tok), jnp.float32),
            jax.ShapeDtypeStruct((DH // 2, tok), jnp.float32),
        ),
        scratch_shapes=[pltpu.VMEM((DH, tok), jnp.float32), pltpu.SemaphoreType.DMA((6,))],
        compiler_params=small,
        name="finish",
    )(total, back, swapped, own_q)
    return (grad_q[None], grad_k.T, grad_v.T)


def solution(mesh):
    placed = (
        P("section", "ctx", None),
        P("ctx", None),
        P("ctx", None),
        P("section", "ctx", None),
        P("ctx"),
    )
    return jax.shard_map(
        on_device,
        mesh=mesh,
        in_specs=placed,
        out_specs=(P("section", "ctx", None), P("ctx", "section"), P("ctx", "section")),
        check_vma=False,
    )
```

```python
import jax
import jax.numpy as jnp
from jax import lax
from jax.experimental import pallas as pl
from jax.experimental.pallas import tpu as pltpu
from jax.sharding import PartitionSpec as P

DH = 128
TOK = 128
RATIO = 5
WIDE = RATIO * DH
ROW = 4
ID_ROWS = 16
SCALE = DH ** (-0.5)
LOG2E = 1.4426950408889634
NEG = -1e30
FAR_FLOPS = 1 << 31
NEAR_FLOPS = 1 << 33
AXES = ("section", "ctx")
NT = (((1,), (1,)), ((), ()))
TN = (((0,), (0,)), ((), ()))


def permuted(x, target):
    sections, cycle = lax.axis_size("section"), lax.axis_size("ctx")
    found = []
    for s in range(sections):
        for c in range(cycle):
            to = target(s, c)
            if 0 <= to[1] < cycle:
                found.append((s * cycle + c, to[0] * cycle + to[1]))
    return lax.ppermute(x, AXES, found)


def shifted(x, by, places=range(ROW)):
    def target(s, c):
        if (c + by) % ROW not in places:
            return (s, -1)
        leaves = c // ROW != (c + by) // ROW
        return ((3 - s // 2) * 2 + s % 2 if leaves else s, c + by)

    return permuted(x, target)


def returned(x):
    def target(s, c):
        share = s // 2
        chip, to = group_of(s % 2, share // 2), c - 1 - share % 2
        return ((3 - chip if c // ROW != to // ROW else chip) * 2 + share % 2, to)

    return permuted(x, target)


def other_core(x):
    return permuted(x, lambda s, c: (s ^ 1, c))


def group_of(core, slot):
    return core + slot * (3 - 2 * core)


def to_owner(x):
    return permuted(x, lambda s, c: (group_of(s % 2, s // 2 // 2) * 2 + s // 2 % 2, c))


def core_groups(core):
    return [group_of(core, slot) for slot in range(2)]


def columns(group, width):
    return pl.ds(pl.multiple_of(group * width, width), width)


def run(copies):
    for copy in copies:
        copy.start()
    for copy in copies:
        copy.wait()


def pack_halo(ids_ref, k_ref, v_ref, out_ref, ids_vmem, sems):
    copies = [pltpu.make_async_copy(ids_ref, ids_vmem, sems.at[4])]
    for slot, group in enumerate(core_groups(lax.axis_index("section") % 2)):
        for i, ref in enumerate((k_ref, v_ref)):
            to = out_ref.at[pl.ds((2 * slot + i) * TOK, TOK)]
            copies.append(pltpu.make_async_copy(ref.at[:, columns(group, DH)], to, sems.at[2 * slot + i]))
    run(copies)
    ids = jnp.broadcast_to((ids_vmem[...] + 1).astype(jnp.float32), (ID_ROWS, TOK))
    out_ref[4 * TOK :] = ids.astype(jnp.bfloat16)


def pack_rows(q_ref, c_ref, out_ref, sems):
    copies = []
    for slot, group in enumerate(core_groups(1 - lax.axis_index("section") % 2)):
        for i, ref in enumerate((q_ref, c_ref)):
            to = out_ref.at[pl.ds(i * TOK, TOK), pl.ds(slot * WIDE, WIDE)]
            copies.append(pltpu.make_async_copy(ref.at[:, columns(group, WIDE)], to, sems.at[2 * slot + i]))
    run(copies)


def halo_mask(ids, *halos):
    first = ids[:, 0:1]
    before = sum(halo[4 * TOK :].astype(jnp.float32)[0:1] for halo in halos)
    held = jnp.sum(jnp.where(before == first + 1.0, 1.0, 0.0), -1, keepdims=True)
    row = lax.broadcasted_iota(jnp.int32, (TOK, TOK), 0).astype(jnp.float32)
    wide = jnp.broadcast_to(ids, (TOK, TOK))
    return jnp.where((wide == first) & (row >= TOK - held), 0.0, NEG)


def mask_near(ids_ref, one_ref, out_ref):
    ids = ids_ref[...].astype(jnp.float32)
    row = lax.broadcasted_iota(jnp.int32, (TOK, TOK), 0)
    col = lax.broadcasted_iota(jnp.int32, (TOK, TOK), 1)
    wide = jnp.broadcast_to(ids, (TOK, TOK))
    out_ref[:TOK] = jnp.where((wide.T == wide) & (row <= col), 0.0, NEG)
    out_ref[TOK:] = halo_mask(ids, one_ref)


def mask_far(ids_ref, two_ref, relay_ref, out_ref):
    out_ref[...] = halo_mask(ids_ref[...].astype(jnp.float32), two_ref, relay_ref)


def attend(
    place_ref, near_ref, far_ref, q_ref, c_ref, oqc_ref, k_ref, v_ref, one_ref, two_ref, relay_ref, dq_ref, odq_ref, part_ref
):
    for slot in range(2):
        attend_slot(
            slot, place_ref, near_ref, far_ref, q_ref, c_ref, oqc_ref, k_ref, v_ref, one_ref, two_ref, relay_ref,
            dq_ref, odq_ref, part_ref,
        )


def attend_slot(
    slot, place_ref, near_ref, far_ref, q_ref, c_ref, oqc_ref, k_ref, v_ref, one_ref, two_ref, relay_ref,
    dq_ref, odq_ref, part_ref,
):
    group = group_of(place_ref[0], slot)

    def lanes(start):
        return pl.ds(pl.multiple_of(start, DH), DH)

    def rows(i):
        return slice((2 * slot + i) * TOK, (2 * slot + i + 1) * TOK)

    keys, values = [
        jnp.concatenate([ref[:, lanes(group * DH)], one_ref[rows(i)], two_ref[rows(i)] + relay_ref[rows(i)]], 0)
        for i, ref in enumerate((k_ref, v_ref))
    ]
    bias = jnp.concatenate([near_ref[...], far_ref[...]], 0)
    queries, cots = [], []
    for h in range(RATIO):
        queries.append(q_ref[:, lanes(group * WIDE + h * DH)])
        cots.append(c_ref[:, lanes(group * WIDE + h * DH)])
    for h in range(RATIO):
        queries.append(oqc_ref[:TOK, lanes(slot * WIDE + h * DH)])
        cots.append(oqc_ref[TOK:, lanes(slot * WIDE + h * DH)])
    queries, cots = jnp.concatenate(queries, 0), jnp.concatenate(cots, 0)
    scores = lax.dot_general(keys, queries, NT, preferred_element_type=jnp.float32)
    grad_probs = lax.dot_general(values, cots, NT, preferred_element_type=jnp.float32)
    probs_low, scaled_low = [], []
    for h in range(2 * RATIO):
        at = slice(h * TOK, (h + 1) * TOK)
        s = scores[:, at] * (SCALE * LOG2E) + bias
        e = jnp.exp2(s - jnp.max(s, 0, keepdims=True))
        p = e * (1.0 / jnp.sum(e, 0, keepdims=True))
        g = grad_probs[:, at]
        dot = jnp.sum(p * g, 0, keepdims=True)
        probs_low.append(p.astype(jnp.bfloat16))
        scaled_low.append((p * (g - dot) * SCALE).astype(jnp.bfloat16))
    probs_low, scaled_low = jnp.concatenate(probs_low, 1), jnp.concatenate(scaled_low, 1)
    grad_v = jnp.dot(probs_low, cots, preferred_element_type=jnp.float32)
    grad_k = jnp.dot(scaled_low, queries, preferred_element_type=jnp.float32)
    grad_q = lax.dot_general(keys, scaled_low, TN, preferred_element_type=jnp.float32).astype(jnp.bfloat16)
    for h in range(2 * RATIO):
        out = dq_ref if h < RATIO else odq_ref
        out[:, lanes(slot * WIDE + h % RATIO * DH)] = grad_q[:, h * TOK : (h + 1) * TOK].T
    half = DH // 2
    grad_k = grad_k.astype(jnp.bfloat16)
    grad_v = grad_v.astype(jnp.bfloat16)
    shares = (
        jnp.concatenate([grad_k[:, :half], grad_v[:, :half]], 1),
        jnp.concatenate([grad_k[:, half:], grad_v[:, half:]], 1),
    )
    for side in range(2):
        part_ref[2 * slot + side, :TOK, :] = shares[side][:TOK]
        for block in (1, 2):
            carrier = 2 * (slot ^ place_ref[1 + block]) + block - 1
            at = slice((1 + side) * TOK, (2 + side) * TOK)
            part_ref[carrier, at, :] = shares[side][block * TOK : (block + 1) * TOK]


def finish(own_ref, back_ref, swapped_ref, own_q_ref, dq_ref, dk_ref, dv_ref, total_ref, sems):
    core = lax.axis_index("section") % 2
    half = DH // 2
    copies = []
    for i, ref in enumerate((own_q_ref, swapped_ref)):
        for slot, group in enumerate(core_groups(core if i == 0 else 1 - core)):
            src = ref.at[:, pl.ds(slot * WIDE, WIDE)]
            copies.append(pltpu.make_async_copy(src, dq_ref.at[:, columns(group, WIDE)], sems.at[2 * i + slot]))
    for copy in copies:
        copy.start()
    mine = back_ref[pl.ds(pl.multiple_of(core * TOK, TOK), TOK), :]
    total = own_ref[...].astype(jnp.float32) + mine.astype(jnp.float32) + swapped_ref[:, 2 * WIDE :].astype(jnp.float32)
    total_ref[...] = total.T
    for i, ref in enumerate((dk_ref, dv_ref)):
        copies.append(pltpu.make_async_copy(total_ref.at[pl.ds(i * half, half)], ref, sems.at[4 + i]))
        copies[-1].start()
    for copy in copies:
        copy.wait()


def on_device(queries, keys, values, cotangent, segment_ids):
    section, me = lax.axis_index("section"), lax.axis_index("ctx")
    core, y_lo = section % 2, section // 2
    tok = keys.shape[0]
    q, c = queries[0], cotangent[0]
    ids = segment_ids.reshape(1, tok)
    hbm = pl.BlockSpec(memory_space=pltpu.HBM)
    vmem = pl.BlockSpec(memory_space=pltpu.VMEM)

    small = pltpu.CompilerParams(vmem_limit_bytes=4 * 1024 * 1024)

    sent = pl.pallas_call(
        pack_halo,
        in_specs=[hbm] * 3,
        out_specs=vmem,
        out_shape=jax.ShapeDtypeStruct((4 * tok + ID_ROWS, DH), jnp.bfloat16),
        scratch_shapes=[pltpu.VMEM((1, tok), jnp.int32), pltpu.SemaphoreType.DMA((5,))],
        compiler_params=small,
        name="pack_halo",
    )(*(pltpu.with_memory_space_constraint(x, pltpu.HBM) for x in (ids, keys, values)))
    one, two = shifted(sent, 1), shifted(sent, 2, (0, 2, 3))
    q, c, _ = lax.optimization_barrier((q, c, sent))
    rows = pl.pallas_call(
        pack_rows,
        in_specs=[hbm] * 2,
        out_specs=vmem,
        out_shape=jax.ShapeDtypeStruct((2 * tok, 2 * WIDE), jnp.bfloat16),
        scratch_shapes=[pltpu.SemaphoreType.DMA((4,))],
        compiler_params=small,
        name="pack_rows",
    )(*(pltpu.with_memory_space_constraint(x, pltpu.HBM) for x in (q, c)))
    near = pl.pallas_call(
        mask_near,
        in_specs=[vmem] * 2,
        out_specs=vmem,
        out_shape=jax.ShapeDtypeStruct((2 * tok, tok), jnp.float32),
        compiler_params=small,
        cost_estimate=pl.CostEstimate(flops=NEAR_FLOPS, bytes_accessed=0, transcendentals=0),
        name="mask_near",
    )(ids, one)
    one, near = lax.optimization_barrier((one, near))
    relay = shifted(one, 1, (1,))
    rows = other_core(rows)
    place = jnp.stack([core, core, (me % ROW < 1).astype(core.dtype), (me % ROW < 2).astype(core.dtype)])
    place = place.astype(jnp.int32)
    far = pl.pallas_call(
        mask_far,
        in_specs=[vmem] * 3,
        out_specs=vmem,
        out_shape=jax.ShapeDtypeStruct((tok, tok), jnp.float32),
        compiler_params=small,
        cost_estimate=pl.CostEstimate(flops=FAR_FLOPS, bytes_accessed=0, transcendentals=0),
        name="mask_far",
    )(ids, two, relay)
    own_q, other_q, part = pl.pallas_call(
        attend,
        in_specs=[pl.BlockSpec(memory_space=pltpu.SMEM)] + [vmem] * 10,
        out_specs=(vmem,) * 3,
        out_shape=(
            jax.ShapeDtypeStruct((tok, 2 * WIDE), jnp.bfloat16),
            jax.ShapeDtypeStruct((tok, 2 * WIDE), jnp.bfloat16),
            jax.ShapeDtypeStruct((4, 3 * tok, DH), jnp.bfloat16),
        ),
        compiler_params=pltpu.CompilerParams(vmem_limit_bytes=24 * 1024 * 1024),
        name="attend",
    )(place, near, far, q, c, rows, keys, values, one, two, relay)
    chips = [[s for s in range(8) if s % 2 == parity] for parity in range(2)]
    shares = lax.all_to_all(part, "section", 0, 0, axis_index_groups=chips)
    back = returned(jnp.sum(shares[:, tok:].astype(jnp.float32), 0).astype(jnp.bfloat16))
    total = to_owner(jnp.sum(shares[:, :tok].astype(jnp.float32), 0).astype(jnp.bfloat16))
    back, total = lax.optimization_barrier((back, total))
    swapped = other_core(jnp.concatenate([other_q, jnp.where(core == 0, back[tok:], back[:tok])], 1))
    grad_q, grad_k, grad_v = pl.pallas_call(
        finish,
        in_specs=[vmem] * 4,
        out_specs=(hbm, hbm, hbm),
        out_shape=(
            jax.ShapeDtypeStruct(q.shape, jnp.bfloat16),
            jax.ShapeDtypeStruct((DH // 2, tok), jnp.float32),
            jax.ShapeDtypeStruct((DH // 2, tok), jnp.float32),
        ),
        scratch_shapes=[pltpu.VMEM((DH, tok), jnp.float32), pltpu.SemaphoreType.DMA((6,))],
        compiler_params=small,
        name="finish",
    )(total, back, swapped, own_q)
    return (grad_q[None], grad_k.T, grad_v.T)


def solution(mesh):
    placed = (
        P("section", "ctx", None),
        P("ctx", None),
        P("ctx", None),
        P("section", "ctx", None),
        P("ctx"),
    )
    return jax.shard_map(
        on_device,
        mesh=mesh,
        in_specs=placed,
        out_specs=(P("section", "ctx", None), P("ctx", "section"), P("ctx", "section")),
        check_vma=False,
    )
```

```python
import jax
import jax.numpy as jnp
from jax import lax
from jax.experimental import pallas as pl
from jax.experimental.pallas import tpu as pltpu
from jax.sharding import PartitionSpec as P

DH = 128
TOK = 128
RATIO = 5
WIDE = RATIO * DH
ROW = 4
ID_ROWS = 16
SCALE = DH ** (-0.5)
LOG2E = 1.4426950408889634
NEG = -1e30
FAR_FLOPS = 1 << 33
NEAR_FLOPS = 1 << 30
ADD_FLOPS = 17 << 27
AXES = ("section", "ctx")
NT = (((1,), (1,)), ((), ()))
TN = (((0,), (0,)), ((), ()))


def permuted(x, target):
    sections, cycle = lax.axis_size("section"), lax.axis_size("ctx")
    found = []
    for s in range(sections):
        for c in range(cycle):
            to = target(s, c)
            if 0 <= to[1] < cycle:
                found.append((s * cycle + c, to[0] * cycle + to[1]))
    return lax.ppermute(x, AXES, found)


def shifted(x, by):
    def target(s, c):
        leaves = c // ROW != (c + by) // ROW
        return ((3 - s // 2) * 2 + s % 2 if leaves else s, c + by)

    return permuted(x, target)


def returned(x):
    def target(s, c):
        share = s // 2
        chip, to = group_of(s % 2, share // 2), c - 1 - share % 2
        return ((3 - chip if c // ROW != to // ROW else chip) * 2 + share % 2, to)

    return permuted(x, target)


def other_core(x):
    return permuted(x, lambda s, c: (s ^ 1, c))


def group_of(core, slot):
    return core + slot * (3 - 2 * core)


def to_owner(x):
    return permuted(x, lambda s, c: (group_of(s % 2, s // 2 // 2) * 2 + s // 2 % 2, c))


def core_groups(core):
    return [group_of(core, slot) for slot in range(2)]


def columns(group, width):
    return pl.ds(pl.multiple_of(group * width, width), width)


def run(copies):
    for copy in copies:
        copy.start()
    for copy in copies:
        copy.wait()


def pack_halo(ids_ref, k_ref, v_ref, out_ref, ids_vmem, sems):
    copies = [pltpu.make_async_copy(ids_ref, ids_vmem, sems.at[4])]
    for slot, group in enumerate(core_groups(lax.axis_index("section") % 2)):
        for i, ref in enumerate((k_ref, v_ref)):
            to = out_ref.at[pl.ds((2 * slot + i) * TOK, TOK)]
            copies.append(pltpu.make_async_copy(ref.at[:, columns(group, DH)], to, sems.at[2 * slot + i]))
    run(copies)
    ids = jnp.broadcast_to((ids_vmem[...] + 1).astype(jnp.float32), (ID_ROWS, TOK))
    out_ref[4 * TOK :] = ids.astype(jnp.bfloat16)


def pack_rows(q_ref, c_ref, out_ref, sems):
    copies = []
    for slot, group in enumerate(core_groups(1 - lax.axis_index("section") % 2)):
        for i, ref in enumerate((q_ref, c_ref)):
            to = out_ref.at[pl.ds(i * TOK, TOK), pl.ds(slot * WIDE, WIDE)]
            copies.append(pltpu.make_async_copy(ref.at[:, columns(group, WIDE)], to, sems.at[2 * slot + i]))
    run(copies)


def halo_mask(ids, halo):
    first = ids[:, 0:1]
    before = halo[4 * TOK :].astype(jnp.float32)[0:1]
    held = jnp.sum(jnp.where(before == first + 1.0, 1.0, 0.0), -1, keepdims=True)
    row = lax.broadcasted_iota(jnp.int32, (TOK, TOK), 0).astype(jnp.float32)
    wide = jnp.broadcast_to(ids, (TOK, TOK))
    return jnp.where((wide == first) & (row >= TOK - held), 0.0, NEG)


def mask_near(ids_ref, one_ref, out_ref):
    ids = ids_ref[...].astype(jnp.float32)
    row = lax.broadcasted_iota(jnp.int32, (TOK, TOK), 0)
    col = lax.broadcasted_iota(jnp.int32, (TOK, TOK), 1)
    wide = jnp.broadcast_to(ids, (TOK, TOK))
    out_ref[:TOK] = jnp.where((wide.T == wide) & (row <= col), 0.0, NEG)
    out_ref[TOK:] = halo_mask(ids, one_ref)


def mask_far(ids_ref, two_ref, out_ref):
    out_ref[...] = halo_mask(ids_ref[...].astype(jnp.float32), two_ref)


def attend(
    place_ref, near_ref, far_ref, q_ref, c_ref, oqc_ref, k_ref, v_ref, one_ref, two_ref, dq_ref, odq_ref, part_ref
):
    for slot in range(2):
        attend_slot(
            slot, place_ref, near_ref, far_ref, q_ref, c_ref, oqc_ref, k_ref, v_ref, one_ref, two_ref,
            dq_ref, odq_ref, part_ref,
        )


def attend_slot(
    slot, place_ref, near_ref, far_ref, q_ref, c_ref, oqc_ref, k_ref, v_ref, one_ref, two_ref,
    dq_ref, odq_ref, part_ref,
):
    group = group_of(place_ref[0], slot)

    def lanes(start):
        return pl.ds(pl.multiple_of(start, DH), DH)

    def rows(i):
        return slice((2 * slot + i) * TOK, (2 * slot + i + 1) * TOK)

    keys, values = [
        jnp.concatenate([ref[:, lanes(group * DH)], one_ref[rows(i)], two_ref[rows(i)]], 0)
        for i, ref in enumerate((k_ref, v_ref))
    ]
    bias = jnp.concatenate([near_ref[...], far_ref[...]], 0)
    queries, cots = [], []
    for h in range(RATIO):
        queries.append(q_ref[:, lanes(group * WIDE + h * DH)])
        cots.append(c_ref[:, lanes(group * WIDE + h * DH)])
    for h in range(RATIO):
        queries.append(oqc_ref[:TOK, lanes(slot * WIDE + h * DH)])
        cots.append(oqc_ref[TOK:, lanes(slot * WIDE + h * DH)])
    queries, cots = jnp.concatenate(queries, 0), jnp.concatenate(cots, 0)
    scores = lax.dot_general(keys, queries, NT, preferred_element_type=jnp.float32)
    grad_probs = lax.dot_general(values, cots, NT, preferred_element_type=jnp.float32)
    probs_low, scaled_low = [], []
    for h in range(2 * RATIO):
        at = slice(h * TOK, (h + 1) * TOK)
        s = scores[:, at] * (SCALE * LOG2E) + bias
        e = jnp.exp2(s - jnp.max(s, 0, keepdims=True))
        p = e * (1.0 / jnp.sum(e, 0, keepdims=True))
        g = grad_probs[:, at]
        dot = jnp.sum(p * g, 0, keepdims=True)
        probs_low.append(p.astype(jnp.bfloat16))
        scaled_low.append((p * (g - dot) * SCALE).astype(jnp.bfloat16))
    probs_low, scaled_low = jnp.concatenate(probs_low, 1), jnp.concatenate(scaled_low, 1)
    grad_v = jnp.dot(probs_low, cots, preferred_element_type=jnp.float32)
    grad_k = jnp.dot(scaled_low, queries, preferred_element_type=jnp.float32)
    grad_q = lax.dot_general(keys, scaled_low, TN, preferred_element_type=jnp.float32).astype(jnp.bfloat16)
    for h in range(2 * RATIO):
        out = dq_ref if h < RATIO else odq_ref
        out[:, lanes(slot * WIDE + h % RATIO * DH)] = grad_q[:, h * TOK : (h + 1) * TOK].T
    half = DH // 2
    grad_k = grad_k.astype(jnp.bfloat16)
    grad_v = grad_v.astype(jnp.bfloat16)
    shares = (
        jnp.concatenate([grad_k[:, :half], grad_v[:, :half]], 1),
        jnp.concatenate([grad_k[:, half:], grad_v[:, half:]], 1),
    )
    for side in range(2):
        part_ref[2 * slot + side, :TOK, :] = shares[side][:TOK]
        for block in (1, 2):
            carrier = 2 * (slot ^ place_ref[1 + block]) + block - 1
            at = slice((1 + side) * TOK, (2 + side) * TOK)
            part_ref[carrier, at, :] = shares[side][block * TOK : (block + 1) * TOK]


def add_up(own_ref, back_ref, swapped_ref, out_ref):
    core = lax.axis_index("section") % 2
    mine = back_ref[pl.ds(pl.multiple_of(core * TOK, TOK), TOK), :]
    out_ref[...] = sum(x.astype(jnp.float32) for x in (own_ref[...], mine, swapped_ref[...])).T


def finish(total_ref, own_q_ref, swapped_ref, dq_ref, dk_ref, dv_ref, sems):
    core = lax.axis_index("section") % 2
    half = DH // 2
    copies = []
    for i, ref in enumerate((own_q_ref, swapped_ref)):
        for slot, group in enumerate(core_groups(core if i == 0 else 1 - core)):
            src = ref.at[:, pl.ds(slot * WIDE, WIDE)]
            copies.append(pltpu.make_async_copy(src, dq_ref.at[:, columns(group, WIDE)], sems.at[2 * i + slot]))
    for i, ref in enumerate((dk_ref, dv_ref)):
        copies.append(pltpu.make_async_copy(total_ref.at[pl.ds(i * half, half)], ref, sems.at[4 + i]))
    run(copies)


def on_device(queries, keys, values, cotangent, segment_ids):
    section, me = lax.axis_index("section"), lax.axis_index("ctx")
    core, y_lo = section % 2, section // 2
    tok = keys.shape[0]
    q, c = queries[0], cotangent[0]
    ids = segment_ids.reshape(1, tok)
    hbm = pl.BlockSpec(memory_space=pltpu.HBM)
    vmem = pl.BlockSpec(memory_space=pltpu.VMEM)

    small = pltpu.CompilerParams(vmem_limit_bytes=4 * 1024 * 1024)

    sent = pl.pallas_call(
        pack_halo,
        in_specs=[hbm] * 3,
        out_specs=vmem,
        out_shape=jax.ShapeDtypeStruct((4 * tok + ID_ROWS, DH), jnp.bfloat16),
        scratch_shapes=[pltpu.VMEM((1, tok), jnp.int32), pltpu.SemaphoreType.DMA((5,))],
        compiler_params=small,
        name="pack_halo",
    )(*(pltpu.with_memory_space_constraint(x, pltpu.HBM) for x in (ids, keys, values)))
    one, two = shifted(sent, 1), shifted(sent, 2)
    q, c, _ = lax.optimization_barrier((q, c, sent))
    rows = pl.pallas_call(
        pack_rows,
        in_specs=[hbm] * 2,
        out_specs=vmem,
        out_shape=jax.ShapeDtypeStruct((2 * tok, 2 * WIDE), jnp.bfloat16),
        scratch_shapes=[pltpu.SemaphoreType.DMA((4,))],
        compiler_params=small,
        name="pack_rows",
    )(*(pltpu.with_memory_space_constraint(x, pltpu.HBM) for x in (q, c)))
    near = pl.pallas_call(
        mask_near,
        in_specs=[vmem] * 2,
        out_specs=vmem,
        out_shape=jax.ShapeDtypeStruct((2 * tok, tok), jnp.float32),
        compiler_params=small,
        cost_estimate=pl.CostEstimate(flops=NEAR_FLOPS, bytes_accessed=0, transcendentals=0),
        name="mask_near",
    )(ids, one)
    rows = other_core(rows)
    place = jnp.stack([core, core, (me % ROW < 1).astype(core.dtype), (me % ROW < 2).astype(core.dtype)])
    place = place.astype(jnp.int32)
    far = pl.pallas_call(
        mask_far,
        in_specs=[vmem] * 2,
        out_specs=vmem,
        out_shape=jax.ShapeDtypeStruct((tok, tok), jnp.float32),
        compiler_params=small,
        cost_estimate=pl.CostEstimate(flops=FAR_FLOPS, bytes_accessed=0, transcendentals=0),
        name="mask_far",
    )(ids, two)
    own_q, other_q, part = pl.pallas_call(
        attend,
        in_specs=[pl.BlockSpec(memory_space=pltpu.SMEM)] + [vmem] * 9,
        out_specs=(vmem,) * 3,
        out_shape=(
            jax.ShapeDtypeStruct((tok, 2 * WIDE), jnp.bfloat16),
            jax.ShapeDtypeStruct((tok, 2 * WIDE), jnp.bfloat16),
            jax.ShapeDtypeStruct((4, 3 * tok, DH), jnp.bfloat16),
        ),
        compiler_params=pltpu.CompilerParams(vmem_limit_bytes=24 * 1024 * 1024),
        name="attend",
    )(place, near, far, q, c, rows, keys, values, one, two)
    chips = [[s for s in range(8) if s % 2 == parity] for parity in range(2)]
    shares = lax.all_to_all(part, "section", 0, 0, axis_index_groups=chips)
    other_q, shares = lax.optimization_barrier((other_q, shares))
    back = returned(jnp.sum(shares[:, tok:].astype(jnp.float32), 0).astype(jnp.bfloat16))
    total = to_owner(jnp.sum(shares[:, :tok].astype(jnp.float32), 0).astype(jnp.bfloat16))
    back, total = lax.optimization_barrier((back, total))
    swapped = other_core(jnp.where(core == 0, back[tok:], back[:tok]))
    swapped_q = other_core(other_q)
    total = pl.pallas_call(
        add_up,
        in_specs=[vmem] * 3,
        out_specs=vmem,
        out_shape=jax.ShapeDtypeStruct((DH, tok), jnp.float32),
        compiler_params=small,
        cost_estimate=pl.CostEstimate(flops=ADD_FLOPS, bytes_accessed=0, transcendentals=0),
        name="add_up",
    )(total, back, swapped)
    grad_q, grad_k, grad_v = pl.pallas_call(
        finish,
        in_specs=[vmem] * 3,
        out_specs=(hbm, hbm, hbm),
        out_shape=(
            jax.ShapeDtypeStruct(q.shape, jnp.bfloat16),
            jax.ShapeDtypeStruct((DH // 2, tok), jnp.float32),
            jax.ShapeDtypeStruct((DH // 2, tok), jnp.float32),
        ),
        scratch_shapes=[pltpu.SemaphoreType.DMA((6,))],
        compiler_params=small,
        name="finish",
    )(total, own_q, swapped_q)
    return (grad_q[None], grad_k.T, grad_v.T)


def solution(mesh):
    placed = (
        P("section", "ctx", None),
        P("ctx", None),
        P("ctx", None),
        P("section", "ctx", None),
        P("ctx"),
    )
    return jax.shard_map(
        on_device,
        mesh=mesh,
        in_specs=placed,
        out_specs=(P("section", "ctx", None), P("ctx", "section"), P("ctx", "section")),
        check_vma=False,
    )
```

```python
import jax
import jax.numpy as jnp
from jax import lax
from jax.experimental import pallas as pl
from jax.experimental.pallas import tpu as pltpu
from jax.sharding import PartitionSpec as P

DH = 128
TOK = 128
RATIO = 5
WIDE = RATIO * DH
ROW = 4
ID_ROWS = 16
SCALE = DH ** (-0.5)
LOG2E = 1.4426950408889634
NEG = -1e30
FAR_FLOPS = 1 << 33
NEAR_FLOPS = 1 << 30
ADD_FLOPS = 17 << 27
AXES = ("section", "ctx")
NT = (((1,), (1,)), ((), ()))
TN = (((0,), (0,)), ((), ()))


def permuted(x, target):
    sections, cycle = lax.axis_size("section"), lax.axis_size("ctx")
    found = []
    for s in range(sections):
        for c in range(cycle):
            to = target(s, c)
            if 0 <= to[1] < cycle:
                found.append((s * cycle + c, to[0] * cycle + to[1]))
    return lax.ppermute(x, AXES, found)


def shifted(x, by):
    def target(s, c):
        leaves = c // ROW != (c + by) // ROW
        crossed = (3 - s // 2) * 2 + s % 2 if by == 1 else s ^ 4
        return (crossed if leaves else s, c + by)

    return permuted(x, target)


def returned(x):
    def target(s, c):
        share = s // 2
        chip, to = group_of(s % 2, share // 2), c - 1 - share % 2
        return ((3 - chip if c // ROW != to // ROW else chip) * 2 + share % 2, to)

    return permuted(x, target)


def other_core(x):
    return permuted(x, lambda s, c: (s ^ 1, c))


def group_of(core, slot):
    return core + slot * (3 - 2 * core)


def to_owner(x):
    return permuted(x, lambda s, c: (group_of(s % 2, s // 2 // 2) * 2 + s // 2 % 2, c))


def core_groups(core):
    return [group_of(core, slot) for slot in range(2)]


def columns(group, width):
    return pl.ds(pl.multiple_of(group * width, width), width)


def run(copies):
    for copy in copies:
        copy.start()
    for copy in copies:
        copy.wait()


def pack_halo(ids_ref, k_ref, v_ref, out_ref, ids_vmem, sems):
    copies = [pltpu.make_async_copy(ids_ref, ids_vmem, sems.at[4])]
    for slot, group in enumerate(core_groups(lax.axis_index("section") % 2)):
        for i, ref in enumerate((k_ref, v_ref)):
            to = out_ref.at[pl.ds((2 * slot + i) * TOK, TOK)]
            copies.append(pltpu.make_async_copy(ref.at[:, columns(group, DH)], to, sems.at[2 * slot + i]))
    run(copies)
    ids = jnp.broadcast_to((ids_vmem[...] + 1).astype(jnp.float32), (ID_ROWS, TOK))
    out_ref[4 * TOK :] = ids.astype(jnp.bfloat16)


def pack_rows(q_ref, c_ref, out_ref, sems):
    copies = []
    for slot, group in enumerate(core_groups(1 - lax.axis_index("section") % 2)):
        for i, ref in enumerate((q_ref, c_ref)):
            to = out_ref.at[pl.ds(i * TOK, TOK), pl.ds(slot * WIDE, WIDE)]
            copies.append(pltpu.make_async_copy(ref.at[:, columns(group, WIDE)], to, sems.at[2 * slot + i]))
    run(copies)


def halo_mask(ids, halo):
    first = ids[:, 0:1]
    before = halo[4 * TOK :].astype(jnp.float32)[0:1]
    held = jnp.sum(jnp.where(before == first + 1.0, 1.0, 0.0), -1, keepdims=True)
    row = lax.broadcasted_iota(jnp.int32, (TOK, TOK), 0).astype(jnp.float32)
    wide = jnp.broadcast_to(ids, (TOK, TOK))
    return jnp.where((wide == first) & (row >= TOK - held), 0.0, NEG)


def mask_near(ids_ref, one_ref, out_ref):
    ids = ids_ref[...].astype(jnp.float32)
    row = lax.broadcasted_iota(jnp.int32, (TOK, TOK), 0)
    col = lax.broadcasted_iota(jnp.int32, (TOK, TOK), 1)
    wide = jnp.broadcast_to(ids, (TOK, TOK))
    out_ref[:TOK] = jnp.where((wide.T == wide) & (row <= col), 0.0, NEG)
    out_ref[TOK:] = halo_mask(ids, one_ref)


def mask_far(ids_ref, two_ref, out_ref):
    out_ref[...] = halo_mask(ids_ref[...].astype(jnp.float32), two_ref)


def attend(
    place_ref, near_ref, far_ref, q_ref, c_ref, oqc_ref, k_ref, v_ref, one_ref, two_ref, dq_ref, odq_ref, part_ref
):
    for slot in range(2):
        attend_slot(
            slot, place_ref, near_ref, far_ref, q_ref, c_ref, oqc_ref, k_ref, v_ref, one_ref, two_ref,
            dq_ref, odq_ref, part_ref,
        )


def attend_slot(
    slot, place_ref, near_ref, far_ref, q_ref, c_ref, oqc_ref, k_ref, v_ref, one_ref, two_ref,
    dq_ref, odq_ref, part_ref,
):
    group = group_of(place_ref[0], slot)

    def lanes(start):
        return pl.ds(pl.multiple_of(start, DH), DH)

    def rows(i):
        return slice((2 * slot + i) * TOK, (2 * slot + i + 1) * TOK)

    keys, values = [
        jnp.concatenate([ref[:, lanes(group * DH)], one_ref[rows(i)], two_ref[rows(i)]], 0)
        for i, ref in enumerate((k_ref, v_ref))
    ]
    bias = jnp.concatenate([near_ref[...], far_ref[...]], 0)
    queries, cots = [], []
    for h in range(RATIO):
        queries.append(q_ref[:, lanes(group * WIDE + h * DH)])
        cots.append(c_ref[:, lanes(group * WIDE + h * DH)])
    for h in range(RATIO):
        queries.append(oqc_ref[:TOK, lanes(slot * WIDE + h * DH)])
        cots.append(oqc_ref[TOK:, lanes(slot * WIDE + h * DH)])
    queries, cots = jnp.concatenate(queries, 0), jnp.concatenate(cots, 0)
    scores = lax.dot_general(keys, queries, NT, preferred_element_type=jnp.float32)
    grad_probs = lax.dot_general(values, cots, NT, preferred_element_type=jnp.float32)
    probs_low, scaled_low = [], []
    for h in range(2 * RATIO):
        at = slice(h * TOK, (h + 1) * TOK)
        s = scores[:, at] * (SCALE * LOG2E) + bias
        e = jnp.exp2(s - jnp.max(s, 0, keepdims=True))
        p = e * (1.0 / jnp.sum(e, 0, keepdims=True))
        g = grad_probs[:, at]
        dot = jnp.sum(p * g, 0, keepdims=True)
        probs_low.append(p.astype(jnp.bfloat16))
        scaled_low.append((p * (g - dot) * SCALE).astype(jnp.bfloat16))
    probs_low, scaled_low = jnp.concatenate(probs_low, 1), jnp.concatenate(scaled_low, 1)
    grad_v = jnp.dot(probs_low, cots, preferred_element_type=jnp.float32)
    grad_k = jnp.dot(scaled_low, queries, preferred_element_type=jnp.float32)
    grad_q = lax.dot_general(keys, scaled_low, TN, preferred_element_type=jnp.float32).astype(jnp.bfloat16)
    for h in range(2 * RATIO):
        out = dq_ref if h < RATIO else odq_ref
        out[:, lanes(slot * WIDE + h % RATIO * DH)] = grad_q[:, h * TOK : (h + 1) * TOK].T
    half = DH // 2
    grad_k = grad_k.astype(jnp.bfloat16)
    grad_v = grad_v.astype(jnp.bfloat16)
    shares = (
        jnp.concatenate([grad_k[:, :half], grad_v[:, :half]], 1),
        jnp.concatenate([grad_k[:, half:], grad_v[:, half:]], 1),
    )
    for side in range(2):
        part_ref[2 * slot + side, :TOK, :] = shares[side][:TOK]
        for block in (1, 2):
            carrier = 2 * (slot ^ place_ref[1 + block]) + block - 1
            at = slice((1 + side) * TOK, (2 + side) * TOK)
            part_ref[carrier, at, :] = shares[side][block * TOK : (block + 1) * TOK]


def add_up(own_ref, back_ref, swapped_ref, out_ref):
    core = lax.axis_index("section") % 2
    mine = back_ref[pl.ds(pl.multiple_of(core * TOK, TOK), TOK), :]
    out_ref[...] = sum(x.astype(jnp.float32) for x in (own_ref[...], mine, swapped_ref[...])).T


def finish(total_ref, own_q_ref, swapped_ref, dq_ref, dk_ref, dv_ref, sems):
    core = lax.axis_index("section") % 2
    half = DH // 2
    copies = []
    for i, ref in enumerate((own_q_ref, swapped_ref)):
        for slot, group in enumerate(core_groups(core if i == 0 else 1 - core)):
            src = ref.at[:, pl.ds(slot * WIDE, WIDE)]
            copies.append(pltpu.make_async_copy(src, dq_ref.at[:, columns(group, WIDE)], sems.at[2 * i + slot]))
    for i, ref in enumerate((dk_ref, dv_ref)):
        copies.append(pltpu.make_async_copy(total_ref.at[pl.ds(i * half, half)], ref, sems.at[4 + i]))
    run(copies)


def on_device(queries, keys, values, cotangent, segment_ids):
    section, me = lax.axis_index("section"), lax.axis_index("ctx")
    core, y_lo = section % 2, section // 2
    tok = keys.shape[0]
    q, c = queries[0], cotangent[0]
    ids = segment_ids.reshape(1, tok)
    hbm = pl.BlockSpec(memory_space=pltpu.HBM)
    vmem = pl.BlockSpec(memory_space=pltpu.VMEM)

    small = pltpu.CompilerParams(vmem_limit_bytes=4 * 1024 * 1024)

    sent = pl.pallas_call(
        pack_halo,
        in_specs=[hbm] * 3,
        out_specs=vmem,
        out_shape=jax.ShapeDtypeStruct((4 * tok + ID_ROWS, DH), jnp.bfloat16),
        scratch_shapes=[pltpu.VMEM((1, tok), jnp.int32), pltpu.SemaphoreType.DMA((5,))],
        compiler_params=small,
        name="pack_halo",
    )(*(pltpu.with_memory_space_constraint(x, pltpu.HBM) for x in (ids, keys, values)))
    one, two = shifted(sent, 1), shifted(sent, 2)
    q, c, _ = lax.optimization_barrier((q, c, sent))
    rows = pl.pallas_call(
        pack_rows,
        in_specs=[hbm] * 2,
        out_specs=vmem,
        out_shape=jax.ShapeDtypeStruct((2 * tok, 2 * WIDE), jnp.bfloat16),
        scratch_shapes=[pltpu.SemaphoreType.DMA((4,))],
        compiler_params=small,
        name="pack_rows",
    )(*(pltpu.with_memory_space_constraint(x, pltpu.HBM) for x in (q, c)))
    near = pl.pallas_call(
        mask_near,
        in_specs=[vmem] * 2,
        out_specs=vmem,
        out_shape=jax.ShapeDtypeStruct((2 * tok, tok), jnp.float32),
        compiler_params=small,
        cost_estimate=pl.CostEstimate(flops=NEAR_FLOPS, bytes_accessed=0, transcendentals=0),
        name="mask_near",
    )(ids, one)
    rows = other_core(rows)
    place = jnp.stack([core, core, (me % ROW < 1).astype(core.dtype), (me % ROW < 2).astype(core.dtype)])
    place = place.astype(jnp.int32)
    far = pl.pallas_call(
        mask_far,
        in_specs=[vmem] * 2,
        out_specs=vmem,
        out_shape=jax.ShapeDtypeStruct((tok, tok), jnp.float32),
        compiler_params=small,
        cost_estimate=pl.CostEstimate(flops=FAR_FLOPS, bytes_accessed=0, transcendentals=0),
        name="mask_far",
    )(ids, two)
    own_q, other_q, part = pl.pallas_call(
        attend,
        in_specs=[pl.BlockSpec(memory_space=pltpu.SMEM)] + [vmem] * 9,
        out_specs=(vmem,) * 3,
        out_shape=(
            jax.ShapeDtypeStruct((tok, 2 * WIDE), jnp.bfloat16),
            jax.ShapeDtypeStruct((tok, 2 * WIDE), jnp.bfloat16),
            jax.ShapeDtypeStruct((4, 3 * tok, DH), jnp.bfloat16),
        ),
        compiler_params=pltpu.CompilerParams(vmem_limit_bytes=24 * 1024 * 1024),
        name="attend",
    )(place, near, far, q, c, rows, keys, values, one, two)
    chips = [[s for s in range(8) if s % 2 == parity] for parity in range(2)]
    shares = lax.all_to_all(part, "section", 0, 0, axis_index_groups=chips)
    other_q, shares = lax.optimization_barrier((other_q, shares))
    back = returned(jnp.sum(shares[:, tok:].astype(jnp.float32), 0).astype(jnp.bfloat16))
    total = to_owner(jnp.sum(shares[:, :tok].astype(jnp.float32), 0).astype(jnp.bfloat16))
    back, total = lax.optimization_barrier((back, total))
    swapped = other_core(jnp.where(core == 0, back[tok:], back[:tok]))
    swapped_q = other_core(other_q)
    total = pl.pallas_call(
        add_up,
        in_specs=[vmem] * 3,
        out_specs=vmem,
        out_shape=jax.ShapeDtypeStruct((DH, tok), jnp.float32),
        compiler_params=small,
        cost_estimate=pl.CostEstimate(flops=ADD_FLOPS, bytes_accessed=0, transcendentals=0),
        name="add_up",
    )(total, back, swapped)
    grad_q, grad_k, grad_v = pl.pallas_call(
        finish,
        in_specs=[vmem] * 3,
        out_specs=(hbm, hbm, hbm),
        out_shape=(
            jax.ShapeDtypeStruct(q.shape, jnp.bfloat16),
            jax.ShapeDtypeStruct((DH // 2, tok), jnp.float32),
            jax.ShapeDtypeStruct((DH // 2, tok), jnp.float32),
        ),
        scratch_shapes=[pltpu.SemaphoreType.DMA((6,))],
        compiler_params=small,
        name="finish",
    )(total, own_q, swapped_q)
    return (grad_q[None], grad_k.T, grad_v.T)


def solution(mesh):
    placed = (
        P("section", "ctx", None),
        P("ctx", None),
        P("ctx", None),
        P("section", "ctx", None),
        P("ctx"),
    )
    return jax.shard_map(
        on_device,
        mesh=mesh,
        in_specs=placed,
        out_specs=(P("section", "ctx", None), P("ctx", "section"), P("ctx", "section")),
        check_vma=False,
    )
```
